256 devices in a mesh: dp: 16 (over x_hi, y, core), tp: 16 (over z, x_lo).
Axes of the slice: x: 4 (x_hi: 2, x_lo: 2; x = x_hi * 2 + x_lo), y: 4, z: 8, core: 2. Of those that a mesh axis runs over, the one named last changes fastest.
Arguments:
- query: bfloat16 [128, 24576], P('dp', 'tp'), may hold values from -10 to 10
- latent_cache: bfloat16 [128, 2048, 576], P('dp'), may hold values from -8 to 8
- lengths: int32 [128], P('dp'), may hold values from 32 to 2048, as said below
- w_uk: bfloat16 [128, 128, 512], P('tp'), may hold values from -0.5 to 0.5
- value_up_weight: bfloat16 [128, 512, 128], P('tp'), may hold values from -0.25 to 0.25
- w_out: bfloat16 [16384, 7168], P('tp', 'dp'), may hold values from -0.046875 to 0.046875
- residual: bfloat16 [128, 7168], P(None, 'dp'), may hold values from -16 to 16
- mlp_norm_scale: bfloat16 [7168], P('dp'), may hold values from 0.099609375 to 1.8984375
- w_gate: bfloat16 [7168, 18432], P('dp', 'tp'), may hold values from -0.0625 to 0.0625
- w_up: bfloat16 [7168, 18432], P('dp', 'tp'), may hold values from -0.0625 to 0.0625
- w_down: bfloat16 [18432, 7168], P('tp', 'dp'), may hold values from -0.046875 to 0.046875
Outputs:
- mixed: bfloat16 [128, 7168], P('tp', 'dp')
The draws below stay inside these ranges and needn't reach their ends.
Inputs may be any that keep to these rules, and one draw needn't show every extreme that they name: `lengths`: some request in every draw has all 2048 slots live.
All inputs are finite; a program needn't handle non-finite values.
Results may differ from the reference program's by a relative error of at most 0.025.
Values may be sent and summed in bfloat16 or wider, within the bound.
A program may use at most 128 MiB of HBM per device.

```python
import jax
import jax.numpy as jnp
from jax import lax

D = 7168
FF = 18432
H = 128
NOPE = 128
ROPE = 64
KVR = 512
VD = 128
L = 2048
B = 128


def draw_query(key, part):
    key = jax.random.fold_in(key, 2)
    first = jax.random.fold_in(key, 0)
    whole = jnp.clip(jax.random.normal(first, (B, H, NOPE + ROPE), jnp.float32), -6.0, 6.0)
    return whole.reshape(B, H * (NOPE + ROPE)).astype(jnp.bfloat16)


def draw_latent_cache(key, part):
    key = jax.random.fold_in(key, 1)
    first, second = jax.random.split(key, 2)
    centre = jax.random.normal(first, (B, 1, KVR), jnp.float32)
    noise = jax.random.normal(second, (B, L, KVR + ROPE), jnp.float32)
    rope_part = noise[:, :, KVR:]
    latent = centre + noise[:, :, :KVR]
    whole = jnp.clip(jnp.concatenate([latent, rope_part], axis=2), -8.0, 8.0)
    return whole.astype(jnp.bfloat16)


def draw_lengths(key, part):
    key = jax.random.fold_in(key, 3)
    first, second, third, fourth = jax.random.split(key, 4)
    short_top = min(512, L)
    short = jax.random.randint(first, (B,), 32, short_top + 1, dtype=jnp.int32)
    long_ones = jax.random.randint(second, (B,), 32, L + 1, dtype=jnp.int32)
    picked = jax.random.randint(third, (B,), 0, 16, dtype=jnp.int32) == 0
    drawn = jnp.where(picked, long_ones, short)
    fullest = jax.random.randint(fourth, (), 0, B, dtype=jnp.int32)
    return jnp.where(jnp.arange(B, dtype=jnp.int32) == fullest, L, drawn).astype(jnp.int32)


def column_scale(low, high):
    position = jnp.arange(D, dtype=jnp.float32) / jnp.float32(max(D - 1, 1))
    return low * jnp.exp(jnp.log(high / low) * position)


def draw_residual(key, part):
    key = jax.random.fold_in(key, 4)
    first, second = jax.random.split(key, 2)
    rough = jax.random.uniform(second, (1, D), jnp.float32, 0.7, 1.3)
    noise = jnp.clip(jax.random.normal(first, (B, D), jnp.float32), -6.0, 6.0)
    whole = noise * rough * column_scale(0.6, 2.0)[None, :]
    return jnp.clip(whole, -16.0, 16.0).astype(jnp.bfloat16)


def levels(own_key, dims, cuts, least, largest):
    def one(axis_at, parts):
        draws = jax.random.uniform(jax.random.fold_in(jax.random.fold_in(own_key, 6), axis_at), (parts,), jnp.float32, least / len(cuts), largest / len(cuts))
        return jnp.repeat(jnp.exp(draws), dims[axis_at] // parts).reshape((-1,) + (1,) * (len(dims) - axis_at - 1))

    gain = one(*cuts[0])
    for cut in cuts[1:]:
        gain = gain * one(*cut)
    return gain


def scatter_about(own_key, dims, scale, most, shards=(), held_as=jnp.bfloat16):
    result = scale * jax.random.normal(own_key, dims, jnp.float32)
    if shards:
        result = result * levels(own_key, dims, shards, -0.22, 0.18)
    return jnp.clip(result, -most, most).astype(held_as)


def setup_inputs(seed: int = 0) -> dict:
    key_list = jax.random.split(jax.random.key(seed), 12)
    query = draw_query(jax.random.fold_in(key_list[11], 71), 0)
    latent_cache = draw_latent_cache(jax.random.fold_in(key_list[11], 71), 0)
    lengths = draw_lengths(jax.random.fold_in(key_list[11], 71), 0)
    w_uk = scatter_about(key_list[3], (H, NOPE, KVR), NOPE ** -0.5, 0.5, ((0, 16),))
    value_up_weight = scatter_about(key_list[4], (H, KVR, VD), KVR ** -0.5, 0.25, ((0, 16),))
    w_out = scatter_about(key_list[5], (H * VD, D), (H * VD) ** -0.5, 0.046875, ((0, 16), (1, 16)))
    residual = draw_residual(jax.random.fold_in(key_list[11], 71), 0)
    mlp_norm_scale = jnp.clip(1.0 + 0.18 * jax.random.normal(key_list[7], (D,), jnp.float32), 0.099609375, 1.8984375).astype(jnp.bfloat16)
    w_gate = scatter_about(key_list[8], (D, FF), D ** -0.5, 0.0625, ((0, 16), (1, 16)))
    w_up = scatter_about(key_list[9], (D, FF), D ** -0.5, 0.0625, ((0, 16), (1, 16)))
    w_down = scatter_about(key_list[10], (FF, D), FF ** -0.5, 0.046875, ((0, 16), (1, 16)))
    return {"query": query, "latent_cache": latent_cache, "lengths": lengths, "w_uk": w_uk, "value_up_weight": value_up_weight, "w_out": w_out, "residual": residual, "mlp_norm_scale": mlp_norm_scale, "w_gate": w_gate, "w_up": w_up, "w_down": w_down}


def attend_one(items, w_latent, value_weight):
    query_row, cache_row, length = items
    head_query = query_row.reshape(H, NOPE + ROPE).astype(jnp.float32)
    q_nope = head_query[:, :NOPE]
    rotary_query = head_query[:, NOPE:]
    q_latent = jnp.einsum('hn,hnk->hk', q_nope, w_latent).astype(jnp.bfloat16)
    latent = cache_row[:, :KVR].astype(jnp.float32)
    rotary_key = cache_row[:, KVR:].astype(jnp.float32)
    scale = 1.0 / jnp.sqrt(jnp.float32(NOPE + ROPE))
    scores = (jnp.einsum('hk,tk->ht', q_latent.astype(jnp.float32), latent) + jnp.einsum('he,te->ht', rotary_query, rotary_key)) * scale
    live = jnp.arange(L, dtype=jnp.int32) < length
    scores = jnp.where(live[None, :], scores, -jnp.inf)
    probs = jax.nn.softmax(scores, axis=-1).astype(jnp.bfloat16)
    attention_context = jnp.einsum('ht,tk->hk', probs.astype(jnp.float32), latent).astype(jnp.bfloat16)
    value_rows = jnp.einsum('fm,fmr->fr', attention_context.astype(jnp.float32), value_weight).astype(jnp.bfloat16)
    return value_rows.reshape(H * VD)

def reference(query, latent_cache, lengths, w_uk, value_up_weight, w_out, residual, mlp_norm_scale, w_gate, w_up, w_down):
    w_latent = w_uk.astype(jnp.float32)
    value_weight = value_up_weight.astype(jnp.float32)
    value_rows = lax.map(lambda items: attend_one(items, w_latent, value_weight), (query, latent_cache, lengths))
    attended = jnp.dot(value_rows, w_out, preferred_element_type=jnp.float32)
    stream = (residual.astype(jnp.float32) + attended).astype(jnp.bfloat16)
    wide = stream.astype(jnp.float32)
    inv_rms = 1.0 / jnp.sqrt(lax.optimization_barrier(jnp.mean(wide * wide, axis=1)) + 1e-06)
    normed = (wide * inv_rms[:, None] * mlp_norm_scale.astype(jnp.float32)[None, :]).astype(jnp.bfloat16)
    gate = jnp.dot(normed, w_gate, preferred_element_type=jnp.float32)
    up = jnp.dot(normed, w_up, preferred_element_type=jnp.float32)
    hidden = (jax.nn.silu(gate) * up).astype(jnp.bfloat16)
    mixed = wide + jnp.dot(hidden, w_down, preferred_element_type=jnp.float32)
    return mixed.astype(jnp.bfloat16)
```

```python
import functools

import jax
import jax.numpy as jnp
from jax import lax
from jax.experimental import pallas as pl
from jax.experimental.pallas import tpu as pltpu
from jax.sharding import PartitionSpec as P

MESH = pl.DeviceIdType.MESH
NOPE = 128
ROPE = 64
KVR = 512
VD = 128
CHUNK = 512
NT = (((1,), (1,)), ((), ()))


def attend_kernel(
    lengths,
    query,
    cache,
    w_uk,
    w_value,
    values,
    held,
    uk_held,
    value_held,
    queries,
    scores,
    top,
    total,
    context,
    cache_sem,
    weight_sem,
):
    requests, heads = queries.shape[0], queries.shape[1]
    uk_copy = pltpu.make_async_copy(w_uk, uk_held, weight_sem.at[0])
    value_copy = pltpu.make_async_copy(w_value, value_held, weight_sem.at[1])
    uk_copy.start()

    def chunk_copy(b, c):
        slots = pl.ds(pl.multiple_of(c * CHUNK, CHUNK), CHUNK)
        return pltpu.make_async_copy(
            cache.at[b, :, slots], held.at[b, :, slots], cache_sem.at[b, c]
        )

    chunks = [lax.div(lengths[b] + (CHUNK - 1), CHUNK) for b in range(requests)]
    for b in range(requests):
        chunk_copy(b, 0).start()
    for b in range(requests):
        pl.loop(1, chunks[b])(lambda c, b=b: chunk_copy(b, c).start())
    value_copy.start()

    uk_copy.wait()
    width = NOPE + ROPE
    for h in range(heads):
        nope = query[:, h * width : h * width + NOPE]
        queries[:, h, :KVR] = jnp.dot(nope, uk_held[h], preferred_element_type=jnp.float32)
        queries[:, h, KVR:] = query[:, h * width + NOPE : (h + 1) * width].astype(jnp.float32)

    scale = 1.0 / jnp.sqrt(jnp.float32(NOPE + ROPE))

    def chunk_scores(b, c):
        slots = pl.ds(pl.multiple_of(c * CHUNK, CHUNK), CHUNK)
        got = jnp.dot(
            queries[b].astype(jnp.bfloat16),
            held[b, :, slots],
            preferred_element_type=jnp.float32,
        )
        at = c * CHUNK + lax.broadcasted_iota(jnp.int32, got.shape, 1)
        got = jnp.where(at < lengths[b], got * scale, -jnp.inf)
        scores[b, :, slots] = got
        return jnp.max(got, axis=1, keepdims=True)

    for b in range(requests):
        chunk_copy(b, 0).wait()
        top[b] = jnp.broadcast_to(chunk_scores(b, 0), top.shape[1:])
    for b in range(requests):

        @pl.loop(1, chunks[b])
        def _(c, b=b):
            chunk_copy(b, c).wait()
            top[b] = jnp.maximum(top[b], chunk_scores(b, c))

    def chunk_context(b, c):
        slots = pl.ds(pl.multiple_of(c * CHUNK, CHUNK), CHUNK)
        probs = jnp.exp(scores[b, :, slots] - top[b, :, :1])
        part = lax.dot_general(
            probs.astype(jnp.bfloat16),
            held[b, :KVR, slots],
            NT,
            preferred_element_type=jnp.float32,
        )
        return part, jnp.sum(probs, axis=1, keepdims=True)

    for b in range(requests):
        part, sums = chunk_context(b, 0)
        context[:, b, :] = part
        total[b] = jnp.broadcast_to(sums, total.shape[1:])
    for b in range(requests):

        @pl.loop(1, chunks[b])
        def _(c, b=b):
            part, sums = chunk_context(b, c)
            context[:, b, :] += part
            total[b] += sums

    for b in range(requests):
        context[:, b, :] = context[:, b, :] / total[b, :, :1]
    value_copy.wait()
    for h in range(heads):
        values[:, h * VD : (h + 1) * VD] = jnp.dot(
            context[h].astype(jnp.bfloat16), value_held[h], preferred_element_type=jnp.float32
        ).astype(jnp.bfloat16)


def attend(query, cache, lengths, w_uk, w_value):
    requests, depth, slots = cache.shape
    heads = w_uk.shape[0]
    vmem = pl.BlockSpec(memory_space=pltpu.VMEM)
    anywhere = pl.BlockSpec(memory_space=pl.ANY)
    return pl.pallas_call(
        attend_kernel,
        out_shape=jax.ShapeDtypeStruct((requests, heads * VD), jnp.bfloat16),
        in_specs=[pl.BlockSpec(memory_space=pltpu.SMEM), vmem, anywhere, anywhere, anywhere],
        out_specs=vmem,
        scratch_shapes=[
            pltpu.VMEM(cache.shape, jnp.bfloat16),
            pltpu.VMEM(w_uk.shape, jnp.bfloat16),
            pltpu.VMEM(w_value.shape, jnp.bfloat16),
            pltpu.VMEM((requests, heads, depth), jnp.float32),
            pltpu.VMEM((requests, heads, slots), jnp.float32),
            pltpu.VMEM((requests, heads, 128), jnp.float32),
            pltpu.VMEM((requests, heads, 128), jnp.float32),
            pltpu.VMEM((heads, requests, KVR), jnp.float32),
            pltpu.SemaphoreType.DMA((requests, slots // CHUNK)),
            pltpu.SemaphoreType.DMA((2,)),
        ],
        compiler_params=pltpu.CompilerParams(vmem_limit_bytes=40 * 2**20),
        name="attend",
    )(lengths, query, cache, w_uk, w_value)


def layer_kernel(
    model,
    values,
    w_out,
    residual,
    gain,
    w_gate,
    w_up,
    w_down,
    mixed,
    out_held,
    gate_held,
    up_held,
    down_held,
    residual_held,
    residual_rows,
    all_values,
    out_send,
    out_recv,
    stream_rows,
    mlp_send,
    mlp_recv,
    hidden_rows,
    down_send,
    down_recv,
    weight_sem,
    send_sem,
    recv_sem,
):
    dp, tp = lax.axis_index("dp"), lax.axis_index("tp")
    groups = all_values.shape[0]
    rows = values.shape[0]
    columns = mixed.shape[1]
    units = gate_held.shape[1]
    wide = out_send.shape[2]

    loads = [
        pltpu.make_async_copy(src, dst, weight_sem.at[at])
        for at, (src, dst) in enumerate(
            [
                (w_out, out_held),
                (residual, residual_held),
                (w_gate, gate_held),
                (w_up, up_held),
                (w_down, down_held),
            ]
        )
    ]
    for load in loads:
        load.start()

    def peer(axis, d):
        me = dp if axis == "dp" else tp
        return lax.rem(me + d, groups)

    barrier = pltpu.get_barrier_semaphore()
    for axis in ("dp", "tp"):

        @pl.loop(1, groups)
        def _(d, axis=axis):
            pl.semaphore_signal(
                barrier, inc=1, device_id={axis: peer(axis, d)}, device_id_type=MESH
            )

    pl.semaphore_wait(barrier, 2 * (groups - 1))

    def exchange(axis, phase, source, target):
        me = dp if axis == "dp" else tp

        def copy(d):
            to = peer(axis, d)
            return pltpu.make_async_remote_copy(
                src_ref=source(to),
                dst_ref=target.at[me],
                send_sem=send_sem.at[phase, to],
                recv_sem=recv_sem.at[phase, me],
                device_id={axis: to},
                device_id_type=MESH,
            )

        @pl.loop(1, groups)
        def _(d):
            copy(d).start()

        def arrive():
            @pl.loop(1, groups)
            def _(d):
                whence = peer(axis, d)
                pltpu.make_async_remote_copy(
                    src_ref=source(whence),
                    dst_ref=target.at[whence],
                    send_sem=send_sem.at[phase, whence],
                    recv_sem=recv_sem.at[phase, whence],
                    device_id={axis: whence},
                    device_id_type=MESH,
                ).wait_recv()

        def sent():
            @pl.loop(1, groups)
            def _(d):
                copy(d).wait_send()

        return arrive, sent

    finish = []

    arrive, sent = exchange("dp", 0, lambda to: values, all_values)
    finish.append(sent)
    all_values[dp] = values[...]
    loads[1].wait()
    residual_rows[...] = residual_held[...].astype(jnp.float32).T
    loads[0].wait()
    arrive()
    attended = lax.dot_general(
        all_values[...].reshape(groups * rows, -1),
        out_held[...],
        NT,
        preferred_element_type=jnp.float32,
    )
    out_send[:, :, :columns] = attended.astype(jnp.bfloat16).reshape(groups, rows, columns)

    arrive, sent = exchange("tp", 1, lambda to: out_send.at[to], out_recv)
    finish.append(sent)
    out_recv[tp] = out_send[tp]
    arrive()
    own = residual_rows[pl.ds(pl.multiple_of(tp * rows, rows), rows), :]
    own = own + jnp.sum(out_recv[:, :, :columns].astype(jnp.float32), axis=0)
    own = own.astype(jnp.bfloat16)
    stream_rows[tp, :, :columns] = own

    arrive, sent = exchange("tp", 2, lambda to: stream_rows.at[tp], stream_rows)
    finish.append(sent)
    loads[2].wait()
    loads[3].wait()
    arrive()
    stream = stream_rows[:, :, :columns].astype(jnp.float32).reshape(groups * rows, columns)
    squares = jnp.sum(stream * stream, axis=1, keepdims=True)
    scaled = (stream * gain[...].astype(jnp.float32)).astype(jnp.bfloat16)
    gate = jnp.dot(scaled, gate_held[...], preferred_element_type=jnp.float32)
    mlp_send[:, :, :units] = gate.astype(jnp.bfloat16).reshape(groups, rows, units)
    up = jnp.dot(scaled, up_held[...], preferred_element_type=jnp.float32)
    mlp_send[:, :, units : 2 * units] = up.astype(jnp.bfloat16).reshape(groups, rows, units)
    high = squares.astype(jnp.bfloat16).astype(jnp.float32)
    lane = lax.broadcasted_iota(jnp.int32, (groups * rows, 128), 1)
    split = jnp.where(lane == 0, high, jnp.where(lane == 1, squares - high, 0.0))
    mlp_send[:, :, 2 * units :] = split.astype(jnp.bfloat16).reshape(groups, rows, 128)

    arrive, sent = exchange("dp", 3, lambda to: mlp_send.at[to], mlp_recv)
    finish.append(sent)
    mlp_recv[dp] = mlp_send[dp]
    arrive()
    sums = jnp.sum(mlp_recv[...].astype(jnp.float32), axis=0)
    squares = sums[:, 2 * units : 2 * units + 1] + sums[:, 2 * units + 1 : 2 * units + 2]
    inv_rms = 1.0 / jnp.sqrt(squares / model + 1e-06)
    gate = sums[:, :units] * inv_rms
    up = sums[:, units : 2 * units] * inv_rms
    hidden = gate / (1.0 + jnp.exp(-gate)) * up
    hidden_rows[dp] = hidden.astype(jnp.bfloat16)

    arrive, sent = exchange("dp", 4, lambda to: hidden_rows.at[dp], hidden_rows)
    finish.append(sent)
    loads[4].wait()
    arrive()
    down = lax.dot_general(
        hidden_rows[...].reshape(groups * rows, units),
        down_held[...],
        NT,
        preferred_element_type=jnp.float32,
    )
    down_send[:, :, :columns] = down.astype(jnp.bfloat16).reshape(groups, rows, columns)

    arrive, sent = exchange("tp", 5, lambda to: down_send.at[to], down_recv)
    finish.append(sent)
    down_recv[tp] = down_send[tp]
    arrive()
    result = jnp.sum(down_recv[:, :, :columns].astype(jnp.float32), axis=0)
    mixed[...] = (own.astype(jnp.float32) + result).astype(jnp.bfloat16)
    for sent in finish:
        sent()


def layer(values, w_out, residual, gain, w_gate, w_up, w_down, groups, model):
    rows, depth = values.shape
    columns, units = w_down.shape
    wide = -(-columns // 128) * 128
    vmem = pl.BlockSpec(memory_space=pltpu.VMEM)
    anywhere = pl.BlockSpec(memory_space=pl.ANY)
    blocks = lambda width: pltpu.VMEM((groups, rows, width), jnp.bfloat16)
    return pl.pallas_call(
        functools.partial(layer_kernel, model),
        out_shape=jax.ShapeDtypeStruct((rows, columns), jnp.bfloat16),
        in_specs=[vmem, anywhere, anywhere, vmem, anywhere, anywhere, anywhere],
        out_specs=vmem,
        scratch_shapes=[
            pltpu.VMEM(w_out.shape, jnp.bfloat16),
            pltpu.VMEM(w_gate.shape, jnp.bfloat16),
            pltpu.VMEM(w_up.shape, jnp.bfloat16),
            pltpu.VMEM(w_down.shape, jnp.bfloat16),
            pltpu.VMEM(residual.shape, jnp.bfloat16),
            pltpu.VMEM(residual.shape[::-1], jnp.float32),
            blocks(depth),
            blocks(wide),
            blocks(wide),
            blocks(wide),
            blocks(2 * units + 128),
            blocks(2 * units + 128),
            blocks(units),
            blocks(wide),
            blocks(wide),
            pltpu.SemaphoreType.DMA((5,)),
            pltpu.SemaphoreType.DMA((6, groups)),
            pltpu.SemaphoreType.DMA((6, groups)),
        ],
        compiler_params=pltpu.CompilerParams(
            collective_id=0, has_side_effects=True, vmem_limit_bytes=40 * 2**20
        ),
        name="layer",
    )(values, w_out, residual, gain, w_gate, w_up, w_down)


def solution(mesh):
    groups = mesh.shape["dp"]

    def on_device(
        query,
        latent_cache,
        lengths,
        w_uk,
        value_up_weight,
        w_out,
        residual,
        mlp_norm_scale,
        w_gate,
        w_up,
        w_down,
    ):
        values = attend(query, jnp.swapaxes(latent_cache, 1, 2), lengths, w_uk, value_up_weight)
        return layer(
            values,
            w_out.T,
            residual.T,
            mlp_norm_scale[None, :],
            w_gate,
            w_up,
            w_down.T,
            groups,
            groups * mlp_norm_scale.shape[0],
        )

    return jax.shard_map(
        on_device,
        mesh=mesh,
        in_specs=(
            P("dp", "tp"),
            P("dp", None, None),
            P("dp"),
            P("tp", None, None),
            P("tp", None, None),
            P("tp", "dp"),
            P(None, "dp"),
            P("dp"),
            P("dp", "tp"),
            P("dp", "tp"),
            P("tp", "dp"),
        ),
        out_specs=P("tp", "dp"),
        check_vma=False,
    )
```

```python
import functools

import jax
import jax.numpy as jnp
from jax import lax
from jax.experimental import pallas as pl
from jax.experimental.pallas import tpu as pltpu
from jax.sharding import PartitionSpec as P

DP_PEERS = sorted(
    [(a, b, c) for a in range(2) for b in range(4) for c in range(2) if a + b + c],
    key=lambda d: -(2 * d[0] + min(d[1], 4 - d[1])),
)
CHIP_PEERS = [d for d in DP_PEERS if d[2] == 0]
TP_PEERS = sorted(
    [(a, b) for a in range(8) for b in range(2) if a + b],
    key=lambda d: -(min(d[0], 8 - d[0]) + d[1]),
)
MESH = pl.DeviceIdType.MESH
NOPE = 128
ROPE = 64
KVR = 512
VD = 128
CHUNK = 512
VMEM_BYTES = 60 * 2**20
NT = (((1,), (1,)), ((), ()))


def attend_kernel(
    lengths_in,
    query_in,
    cache,
    w_uk,
    w_value,
    values,
    lengths,
    query,
    held,
    uk_held,
    value_held,
    queries,
    scores,
    top,
    total,
    context,
    cache_sem,
    weight_sem,
):
    requests, heads = queries.shape[0], queries.shape[1]
    uk_copy = pltpu.make_async_copy(w_uk, uk_held, weight_sem.at[0])
    value_copy = pltpu.make_async_copy(w_value, value_held, weight_sem.at[1])
    lengths_copy = pltpu.make_async_copy(lengths_in, lengths, weight_sem.at[2])
    query_copy = pltpu.make_async_copy(query_in, query, weight_sem.at[3])
    lengths_copy.start()
    query_copy.start()
    uk_copy.start()

    def chunk_copy(b, c):
        slots = pl.ds(pl.multiple_of(c * CHUNK, CHUNK), CHUNK)
        return pltpu.make_async_copy(
            cache.at[b, :, slots], held.at[b, :, slots], cache_sem.at[b, c]
        )

    for b in range(requests):
        chunk_copy(b, 0).start()
    lengths_copy.wait()
    chunks = [lax.div(lengths[b] + (CHUNK - 1), CHUNK) for b in range(requests)]
    for b in range(requests):
        pl.loop(1, chunks[b])(lambda c, b=b: chunk_copy(b, c).start())
    value_copy.start()

    query_copy.wait()
    uk_copy.wait()
    width = NOPE + ROPE
    for h in range(heads):
        nope = query[:, h * width : h * width + NOPE]
        queries[:, h, :KVR] = jnp.dot(nope, uk_held[h], preferred_element_type=jnp.float32)
        queries[:, h, KVR:] = query[:, h * width + NOPE : (h + 1) * width].astype(jnp.float32)

    scale = 1.0 / jnp.sqrt(jnp.float32(NOPE + ROPE))

    def chunk_scores(b, c):
        slots = pl.ds(pl.multiple_of(c * CHUNK, CHUNK), CHUNK)
        got = jnp.dot(
            queries[b].astype(jnp.bfloat16),
            held[b, :, slots],
            preferred_element_type=jnp.float32,
        )
        at = c * CHUNK + lax.broadcasted_iota(jnp.int32, got.shape, 1)
        got = jnp.where(at < lengths[b], got * scale, -jnp.inf)
        scores[b, :, slots] = got
        return jnp.max(got, axis=1, keepdims=True)

    for b in range(requests):
        chunk_copy(b, 0).wait()
        top[b] = jnp.broadcast_to(chunk_scores(b, 0), top.shape[1:])
    for b in range(requests):

        @pl.loop(1, chunks[b])
        def _(c, b=b):
            chunk_copy(b, c).wait()
            top[b] = jnp.maximum(top[b], chunk_scores(b, c))

    def chunk_context(b, c):
        slots = pl.ds(pl.multiple_of(c * CHUNK, CHUNK), CHUNK)
        probs = jnp.exp(scores[b, :, slots] - top[b, :, :1])
        part = lax.dot_general(
            probs.astype(jnp.bfloat16),
            held[b, :KVR, slots],
            NT,
            preferred_element_type=jnp.float32,
        )
        return part, jnp.sum(probs, axis=1, keepdims=True)

    for b in range(requests):
        part, sums = chunk_context(b, 0)
        context[:, b, :] = part
        total[b] = jnp.broadcast_to(sums, total.shape[1:])
    for b in range(requests):

        @pl.loop(1, chunks[b])
        def _(c, b=b):
            part, sums = chunk_context(b, c)
            context[:, b, :] += part
            total[b] += sums

    for b in range(requests):
        context[:, b, :] = context[:, b, :] / total[b, :, :1]
    value_copy.wait()
    for h in range(heads):
        values[:, h * VD : (h + 1) * VD] = jnp.dot(
            context[h].astype(jnp.bfloat16), value_held[h], preferred_element_type=jnp.float32
        ).astype(jnp.bfloat16)


def attend(query, cache, lengths, w_uk, w_value):
    requests, depth, slots = cache.shape
    heads = w_uk.shape[0]
    vmem = pl.BlockSpec(memory_space=pltpu.VMEM)
    anywhere = pl.BlockSpec(memory_space=pl.ANY)
    return pl.pallas_call(
        attend_kernel,
        out_shape=jax.ShapeDtypeStruct((requests, heads * VD), jnp.bfloat16),
        in_specs=[anywhere] * 5,
        out_specs=vmem,
        scratch_shapes=[
            pltpu.SMEM(lengths.shape, jnp.int32),
            pltpu.VMEM(query.shape, jnp.bfloat16),
            pltpu.VMEM(cache.shape, jnp.bfloat16),
            pltpu.VMEM(w_uk.shape, jnp.bfloat16),
            pltpu.VMEM(w_value.shape, jnp.bfloat16),
            pltpu.VMEM((requests, heads, depth), jnp.float32),
            pltpu.VMEM((requests, heads, slots), jnp.float32),
            pltpu.VMEM((requests, heads, 128), jnp.float32),
            pltpu.VMEM((requests, heads, 128), jnp.float32),
            pltpu.VMEM((heads, requests, KVR), jnp.float32),
            pltpu.SemaphoreType.DMA((requests, slots // CHUNK)),
            pltpu.SemaphoreType.DMA((4,)),
        ],
        compiler_params=pltpu.CompilerParams(vmem_limit_bytes=VMEM_BYTES),
        name="attend",
    )(lengths, query, cache, w_uk, w_value)


def layer_kernel(
    model,
    values,
    w_out,
    residual,
    gain_in,
    w_gate,
    w_up,
    w_down,
    mixed,
    out_held,
    gate_held,
    up_held,
    down_held,
    residual_held,
    gain,
    residual_rows,
    all_values,
    out_send,
    out_recv,
    stream_rows,
    gate_pair,
    gate_other,
    gate_send,
    gate_recv,
    up_pair,
    up_other,
    up_send,
    up_recv,
    hidden_rows,
    down_send,
    down_recv,
    weight_sem,
    send_sem,
    recv_sem,
):
    dp, tp = lax.axis_index("dp"), lax.axis_index("tp")
    groups = all_values.shape[0]
    rows = values.shape[0]
    columns = mixed.shape[1]
    units = gate_held.shape[1]

    loads = [
        pltpu.make_async_copy(src, dst, weight_sem.at[at])
        for at, (src, dst) in enumerate(
            [
                (w_out, out_held),
                (residual, residual_held),
                (gain_in, gain),
                (w_gate, gate_held),
                (w_up, up_held),
                (w_down, down_held),
            ]
        )
    ]
    for load in loads:
        load.start()

    core, y, x_hi = lax.rem(dp, 2), lax.rem(dp // 2, 4), dp // 8
    x_lo, z = lax.rem(tp, 2), tp // 2

    def peer(axis, d):
        if axis == "dp":
            return (
                lax.rem(x_hi + d[0], 2) * 8 + lax.rem(y + d[1], 4) * 2 + lax.rem(core + d[2], 2)
            )
        return lax.rem(z + d[0], 8) * 2 + lax.rem(x_lo + d[1], 2)

    barrier = pltpu.get_barrier_semaphore()
    for axis, peers in (("dp", DP_PEERS), ("tp", TP_PEERS)):
        for d in peers:
            pl.semaphore_signal(
                barrier, inc=1, device_id={axis: peer(axis, d)}, device_id_type=MESH
            )
    pl.semaphore_wait(barrier, len(DP_PEERS) + len(TP_PEERS))

    finish = []

    def exchange(axis, phase, peers, source, target, place):
        for d in peers:
            to = peer(axis, d)
            pltpu.make_async_remote_copy(
                src_ref=source(to),
                dst_ref=target.at[place],
                send_sem=send_sem.at[phase],
                recv_sem=recv_sem.at[phase],
                device_id={axis: to},
                device_id_type=MESH,
            ).start()
        blocks = target.at[: len(peers)]
        finish.append(pltpu.make_async_copy(blocks, blocks, send_sem.at[phase]).wait)
        return pltpu.make_async_copy(blocks, blocks, recv_sem.at[phase]).wait

    arrive = exchange("dp", 0, DP_PEERS, lambda to: values, all_values, dp)
    all_values[dp] = values[...]
    loads[1].wait()
    residual_rows[...] = residual_held[...].astype(jnp.float32).T
    loads[0].wait()
    arrive()
    attended = lax.dot_general(
        all_values[...].reshape(groups * rows, -1),
        out_held[...],
        NT,
        preferred_element_type=jnp.float32,
    )
    out_send[:, :, :columns] = attended.astype(jnp.bfloat16).reshape(groups, rows, columns)

    arrive = exchange("tp", 1, TP_PEERS, lambda to: out_send.at[to], out_recv, tp)
    out_recv[tp] = out_send[tp]
    arrive()
    own = residual_rows[pl.ds(pl.multiple_of(tp * rows, rows), rows), :]
    own = own + jnp.sum(out_recv[:, :, :columns].astype(jnp.float32), axis=0)
    own = own.astype(jnp.bfloat16)
    stream_rows[tp, :, :columns] = own

    arrive = exchange("tp", 2, TP_PEERS, lambda to: stream_rows.at[tp], stream_rows, tp)
    loads[2].wait()
    loads[3].wait()
    loads[4].wait()
    arrive()
    stream = stream_rows[:, :, :columns].astype(jnp.float32).reshape(groups * rows, columns)
    squares = jnp.sum(stream * stream, axis=1, keepdims=True)
    scaled = (stream * gain[...].astype(jnp.float32)[None, :]).astype(jnp.bfloat16)
    high = squares.astype(jnp.bfloat16).astype(jnp.float32)
    lane = lax.broadcasted_iota(jnp.int32, (groups * rows, 128), 1)
    split = jnp.where(lane == 0, high, jnp.where(lane == 1, squares - high, 0.0))

    def swap(part, wide, pair_send, pair_recv):
        chips = groups // 2
        blocks = wide.astype(jnp.bfloat16).reshape(chips, 2, rows, -1)
        pair_send[0] = blocks[:, 0]
        pair_send[1] = blocks[:, 1]
        copy = pltpu.make_async_remote_copy(
            src_ref=pair_send.at[1 - core],
            dst_ref=pair_recv,
            send_sem=send_sem.at[5 + part],
            recv_sem=recv_sem.at[5 + part],
            device_id={"dp": peer("dp", (0, 0, 1))},
            device_id_type=MESH,
        )
        copy.start()
        return copy

    gate = jnp.dot(scaled, gate_held[...], preferred_element_type=jnp.float32)
    gate_copy = swap(0, gate, gate_pair, gate_other)
    up = jnp.dot(scaled, up_held[...], preferred_element_type=jnp.float32)
    up = jnp.concatenate([up, split], axis=1)
    up_copy = swap(1, up, up_pair, up_other)

    def scatter(part, copy, pair_send, pair_recv, send, recv):
        copy.wait_recv()
        finish.append(copy.wait_send)
        both = pair_send[core].astype(jnp.float32) + pair_recv[...].astype(jnp.float32)
        send[...] = both.astype(jnp.bfloat16)
        arrive = exchange(
            "dp", 7 + part, CHIP_PEERS, lambda to: send.at[to // 2], recv, dp // 2
        )
        recv[dp // 2] = send[dp // 2]
        return arrive

    gate_arrive = scatter(0, gate_copy, gate_pair, gate_other, gate_send, gate_recv)
    up_arrive = scatter(1, up_copy, up_pair, up_other, up_send, up_recv)
    gate_arrive()
    gate = jnp.sum(gate_recv[...].astype(jnp.float32), axis=0)
    up_arrive()
    up = jnp.sum(up_recv[...].astype(jnp.float32), axis=0)
    squares = up[:, units : units + 1] + up[:, units + 1 : units + 2]
    inv_rms = 1.0 / jnp.sqrt(squares / model + 1e-06)
    gate = gate * inv_rms
    up = up[:, :units] * inv_rms
    hidden = gate / (1.0 + jnp.exp(-gate)) * up
    hidden_rows[dp] = hidden.astype(jnp.bfloat16)

    arrive = exchange("dp", 3, DP_PEERS, lambda to: hidden_rows.at[dp], hidden_rows, dp)
    loads[5].wait()
    arrive()
    down = lax.dot_general(
        hidden_rows[...].reshape(groups * rows, units),
        down_held[...],
        NT,
        preferred_element_type=jnp.float32,
    )
    down_send[:, :, :columns] = down.astype(jnp.bfloat16).reshape(groups, rows, columns)

    arrive = exchange("tp", 4, TP_PEERS, lambda to: down_send.at[to], down_recv, tp)
    down_recv[tp] = down_send[tp]
    arrive()
    result = jnp.sum(down_recv[:, :, :columns].astype(jnp.float32), axis=0)
    mixed[...] = (own.astype(jnp.float32) + result).astype(jnp.bfloat16)
    for sent in finish:
        sent()


def layer(values, w_out, residual, gain, w_gate, w_up, w_down, groups, model):
    rows, depth = values.shape
    columns, units = w_down.shape
    wide = -(-columns // 128) * 128
    vmem = pl.BlockSpec(memory_space=pltpu.VMEM)
    anywhere = pl.BlockSpec(memory_space=pl.ANY)
    blocks = lambda width: pltpu.VMEM((groups, rows, width), jnp.bfloat16)
    half = lambda width: pltpu.VMEM((groups // 2, rows, width), jnp.bfloat16)
    pair = lambda width: pltpu.VMEM((2, groups // 2, rows, width), jnp.bfloat16)
    return pl.pallas_call(
        functools.partial(layer_kernel, model),
        out_shape=jax.ShapeDtypeStruct((rows, columns), jnp.bfloat16),
        in_specs=[vmem] + [anywhere] * 6,
        out_specs=vmem,
        scratch_shapes=[
            pltpu.VMEM(w_out.shape, jnp.bfloat16),
            pltpu.VMEM(w_gate.shape, jnp.bfloat16),
            pltpu.VMEM(w_up.shape, jnp.bfloat16),
            pltpu.VMEM(w_down.shape, jnp.bfloat16),
            pltpu.VMEM(residual.shape, jnp.bfloat16),
            pltpu.VMEM(gain.shape, jnp.bfloat16),
            pltpu.VMEM(residual.shape[::-1], jnp.float32),
            blocks(depth),
            blocks(wide),
            blocks(wide),
            blocks(wide),
            pair(units),
            half(units),
            half(units),
            half(units),
            pair(units + 128),
            half(units + 128),
            half(units + 128),
            half(units + 128),
            blocks(units),
            blocks(wide),
            blocks(wide),
            pltpu.SemaphoreType.DMA((6,)),
            pltpu.SemaphoreType.DMA((9,)),
            pltpu.SemaphoreType.DMA((9,)),
        ],
        compiler_params=pltpu.CompilerParams(
            collective_id=0, has_side_effects=True, vmem_limit_bytes=VMEM_BYTES
        ),
        name="layer",
    )(values, w_out, residual, gain, w_gate, w_up, w_down)


def solution(mesh):
    groups = mesh.shape["dp"]

    def on_device(
        query,
        latent_cache,
        lengths,
        w_uk,
        value_up_weight,
        w_out,
        residual,
        mlp_norm_scale,
        w_gate,
        w_up,
        w_down,
    ):
        values = attend(query, jnp.swapaxes(latent_cache, 1, 2), lengths, w_uk, value_up_weight)
        return layer(
            values,
            w_out.T,
            residual.T,
            mlp_norm_scale,
            w_gate,
            w_up,
            w_down.T,
            groups,
            groups * mlp_norm_scale.shape[0],
        )

    return jax.shard_map(
        on_device,
        mesh=mesh,
        in_specs=(
            P("dp", "tp"),
            P("dp", None, None),
            P("dp"),
            P("tp", None, None),
            P("tp", None, None),
            P("tp", "dp"),
            P(None, "dp"),
            P("dp"),
            P("dp", "tp"),
            P("dp", "tp"),
            P("tp", "dp"),
        ),
        out_specs=P("tp", "dp"),
        check_vma=False,
    )
```

```python
import functools

import jax
import jax.numpy as jnp
from jax import lax
from jax.experimental import pallas as pl
from jax.experimental.pallas import tpu as pltpu
from jax.sharding import PartitionSpec as P

DP_PEERS = sorted(
    [(a, b, c) for a in range(2) for b in range(4) for c in range(2) if a + b + c],
    key=lambda d: -(2 * d[0] + min(d[1], 4 - d[1])),
)
CHIP_PEERS = [d for d in DP_PEERS if d[2] == 0]
TP_PEERS = sorted(
    [(a, b) for a in range(8) for b in range(2) if a + b],
    key=lambda d: -(min(d[0], 8 - d[0]) + d[1]),
)
MESH = pl.DeviceIdType.MESH
NOPE = 128
ROPE = 64
KVR = 512
VD = 128
FIRST = 512
VMEM_BYTES = 60 * 2**20
NT = (((1,), (1,)), ((), ()))


def project(query, w_uk, queries):
    width = NOPE + ROPE
    for h in range(w_uk.shape[0]):
        nope = query[:, h * width : h * width + NOPE]
        queries[:, h, :KVR] = jnp.dot(nope, w_uk[h], preferred_element_type=jnp.float32)
        queries[:, h, KVR:] = query[:, h * width + NOPE : (h + 1) * width].astype(jnp.float32)


def live_scores(query, keys, first, length):
    got = jnp.dot(query.astype(jnp.bfloat16), keys, preferred_element_type=jnp.float32)
    at = first + lax.broadcasted_iota(jnp.int32, got.shape, 1)
    return jnp.where(at < length, got * (1.0 / jnp.sqrt(jnp.float32(NOPE + ROPE))), -jnp.inf)


def weighted(probs, keys):
    return lax.dot_general(
        probs.astype(jnp.bfloat16), keys, NT, preferred_element_type=jnp.float32
    )


def later_kernel(
    lengths_in,
    query_in,
    cache,
    w_uk,
    sums,
    stats,
    lengths,
    query,
    held,
    uk_held,
    queries,
    cache_sem,
    load_sem,
):
    requests = queries.shape[0]
    most = cache.shape[2] // FIRST - 1
    loads = [
        pltpu.make_async_copy(src, dst, load_sem.at[at])
        for at, (src, dst) in enumerate(
            [(lengths_in, lengths), (w_uk, uk_held), (query_in, query)]
        )
    ]
    for load in loads:
        load.start()
    sums[...] = jnp.zeros_like(sums)
    stats[0] = jnp.full(stats.shape[1:], -1e30, jnp.float32)
    stats[1] = jnp.zeros(stats.shape[1:], jnp.float32)
    loads[0].wait()

    def each(step):
        @pl.loop(0, requests)
        def _(b):
            chunks = lax.div(lengths[b] - 1, FIRST)
            for k in range(1, most + 1):
                pl.when(chunks == k)(lambda k=k: step(b, k * FIRST))

    def copy(b, width):
        return pltpu.make_async_copy(
            cache.at[b, :, FIRST : FIRST + width], held.at[b, :, :width], cache_sem.at[b]
        )

    each(lambda b, width: copy(b, width).start())
    loads[1].wait()
    loads[2].wait()
    longest = lengths[0]
    for b in range(1, requests):
        longest = jnp.maximum(longest, lengths[b])

    @pl.when(longest > FIRST)
    def _():
        project(query, uk_held, queries)

        def step(b, width):
            copy(b, width).wait()
            scores = live_scores(queries[b], held[b, :, :width], FIRST, lengths[b])
            top = jnp.max(scores, axis=1, keepdims=True)
            probs = jnp.exp(scores - top)
            total = jnp.sum(probs, axis=1, keepdims=True)
            sums[b] = weighted(probs, held[b, :KVR, :width])
            stats[0, b] = jnp.broadcast_to(top, stats.shape[2:])
            stats[1, b] = jnp.broadcast_to(total, stats.shape[2:])

        each(step)


def attend_later(query, cache, lengths, w_uk):
    requests, depth, slots = cache.shape
    heads = w_uk.shape[0]
    vmem = pl.BlockSpec(memory_space=pltpu.VMEM)
    anywhere = pl.BlockSpec(memory_space=pl.ANY)
    return pl.pallas_call(
        later_kernel,
        out_shape=[
            jax.ShapeDtypeStruct((requests, heads, KVR), jnp.float32),
            jax.ShapeDtypeStruct((2, requests, heads, 128), jnp.float32),
        ],
        in_specs=[anywhere] * 4,
        out_specs=[vmem] * 2,
        scratch_shapes=[
            pltpu.SMEM(lengths.shape, jnp.int32),
            pltpu.VMEM(query.shape, jnp.bfloat16),
            pltpu.VMEM((requests, depth, slots - FIRST), jnp.bfloat16),
            pltpu.VMEM(w_uk.shape, jnp.bfloat16),
            pltpu.VMEM((requests, heads, depth), jnp.float32),
            pltpu.SemaphoreType.DMA((requests,)),
            pltpu.SemaphoreType.DMA((3,)),
        ],
        compiler_params=pltpu.CompilerParams(vmem_limit_bytes=VMEM_BYTES),
        name="attend_later",
    )(lengths, query, cache, w_uk)


def layer_kernel(
    model,
    lengths_in,
    query_in,
    cache,
    w_uk,
    w_value,
    sums_in,
    stats_in,
    w_out,
    residual,
    gain_in,
    w_gate,
    w_up,
    w_down,
    mixed,
    lengths,
    query,
    held,
    uk_held,
    value_held,
    sums,
    stats,
    queries,
    scores,
    context,
    values,
    out_held,
    gate_held,
    up_held,
    down_held,
    residual_held,
    gain,
    residual_rows,
    all_values,
    out_send,
    out_recv,
    stream_rows,
    gate_pair,
    gate_other,
    gate_send,
    gate_recv,
    up_pair,
    up_other,
    up_send,
    up_recv,
    hidden_rows,
    down_send,
    down_recv,
    attend_sem,
    cache_sem,
    weight_sem,
    send_sem,
    recv_sem,
):
    dp, tp = lax.axis_index("dp"), lax.axis_index("tp")
    groups = all_values.shape[0]
    rows = values.shape[0]
    columns = mixed.shape[1]
    units = gate_held.shape[1]

    requests = cache.shape[0]
    attend_loads = [
        pltpu.make_async_copy(src, dst, attend_sem.at[at])
        for at, (src, dst) in enumerate(
            [
                (w_uk, uk_held),
                (query_in, query),
                (lengths_in, lengths),
                (sums_in, sums),
                (stats_in, stats),
                (w_value, value_held),
            ]
        )
    ]
    cache_loads = [
        pltpu.make_async_copy(cache.at[b, :, :FIRST], held.at[b], cache_sem.at[b])
        for b in range(requests)
    ]
    loads = [
        pltpu.make_async_copy(src, dst, weight_sem.at[at])
        for at, (src, dst) in enumerate(
            [
                (w_out, out_held),
                (residual, residual_held),
                (gain_in, gain),
                (w_gate, gate_held),
                (w_up, up_held),
                (w_down, down_held),
            ]
        )
    ]
    for load in attend_loads[:3] + cache_loads + attend_loads[3:] + loads:
        load.start()

    core, y, x_hi = lax.rem(dp, 2), lax.rem(dp // 2, 4), dp // 8
    x_lo, z = lax.rem(tp, 2), tp // 2

    def peer(axis, d):
        if axis == "dp":
            return (
                lax.rem(x_hi + d[0], 2) * 8 + lax.rem(y + d[1], 4) * 2 + lax.rem(core + d[2], 2)
            )
        return lax.rem(z + d[0], 8) * 2 + lax.rem(x_lo + d[1], 2)

    barrier = pltpu.get_barrier_semaphore()
    for axis, peers in (("dp", DP_PEERS), ("tp", TP_PEERS)):
        for d in peers:
            pl.semaphore_signal(
                barrier, inc=1, device_id={axis: peer(axis, d)}, device_id_type=MESH
            )

    for load in attend_loads[:3]:
        load.wait()
    project(query, uk_held, queries)
    for b in range(requests):
        cache_loads[b].wait()
        scores[b] = live_scores(queries[b], held[b], 0, lengths[b])
    for load in attend_loads[3:]:
        load.wait()
    for b in range(requests):
        later = stats[0, b, :, :1]
        top = jnp.maximum(jnp.max(scores[b], axis=1, keepdims=True), later)
        share = jnp.exp(later - top)
        probs = jnp.exp(scores[b] - top)
        total = jnp.sum(probs, axis=1, keepdims=True) + stats[1, b, :, :1] * share
        context[:, b, :] = (weighted(probs, held[b, :KVR, :]) + sums[b] * share) / total
    for h in range(value_held.shape[0]):
        values[:, h * VD : (h + 1) * VD] = jnp.dot(
            context[h].astype(jnp.bfloat16), value_held[h], preferred_element_type=jnp.float32
        ).astype(jnp.bfloat16)

    pl.semaphore_wait(barrier, len(DP_PEERS) + len(TP_PEERS))
    finish = []

    def exchange(axis, phase, peers, source, target, place):
        for d in peers:
            to = peer(axis, d)
            pltpu.make_async_remote_copy(
                src_ref=source(to),
                dst_ref=target.at[place],
                send_sem=send_sem.at[phase],
                recv_sem=recv_sem.at[phase],
                device_id={axis: to},
                device_id_type=MESH,
            ).start()
        blocks = target.at[: len(peers)]
        finish.append(pltpu.make_async_copy(blocks, blocks, send_sem.at[phase]).wait)
        return pltpu.make_async_copy(blocks, blocks, recv_sem.at[phase]).wait

    arrive = exchange("dp", 0, DP_PEERS, lambda to: values, all_values, dp)
    all_values[dp] = values[...]
    loads[1].wait()
    residual_rows[...] = residual_held[...].astype(jnp.float32).T
    loads[0].wait()
    arrive()
    attended = lax.dot_general(
        all_values[...].reshape(groups * rows, -1),
        out_held[...],
        NT,
        preferred_element_type=jnp.float32,
    )
    out_send[:, :, :columns] = attended.astype(jnp.bfloat16).reshape(groups, rows, columns)

    arrive = exchange("tp", 1, TP_PEERS, lambda to: out_send.at[to], out_recv, tp)
    out_recv[tp] = out_send[tp]
    arrive()
    own = residual_rows[pl.ds(pl.multiple_of(tp * rows, rows), rows), :]
    own = own + jnp.sum(out_recv[:, :, :columns].astype(jnp.float32), axis=0)
    own = own.astype(jnp.bfloat16)
    stream_rows[tp, :, :columns] = own

    arrive = exchange("tp", 2, TP_PEERS, lambda to: stream_rows.at[tp], stream_rows, tp)
    loads[2].wait()
    loads[3].wait()
    loads[4].wait()
    arrive()
    stream = stream_rows[:, :, :columns].astype(jnp.float32).reshape(groups * rows, columns)
    squares = jnp.sum(stream * stream, axis=1, keepdims=True)
    scaled = (stream * gain[...].astype(jnp.float32)[None, :]).astype(jnp.bfloat16)
    high = squares.astype(jnp.bfloat16).astype(jnp.float32)
    lane = lax.broadcasted_iota(jnp.int32, (groups * rows, 128), 1)
    split = jnp.where(lane == 0, high, jnp.where(lane == 1, squares - high, 0.0))

    def swap(part, wide, pair_send, pair_recv):
        chips = groups // 2
        blocks = wide.astype(jnp.bfloat16).reshape(chips, 2, rows, -1)
        pair_send[0] = blocks[:, 0]
        pair_send[1] = blocks[:, 1]
        copy = pltpu.make_async_remote_copy(
            src_ref=pair_send.at[1 - core],
            dst_ref=pair_recv,
            send_sem=send_sem.at[5 + part],
            recv_sem=recv_sem.at[5 + part],
            device_id={"dp": peer("dp", (0, 0, 1))},
            device_id_type=MESH,
        )
        copy.start()
        return copy

    gate = jnp.dot(scaled, gate_held[...], preferred_element_type=jnp.float32)
    gate_copy = swap(0, gate, gate_pair, gate_other)
    up = jnp.dot(scaled, up_held[...], preferred_element_type=jnp.float32)
    up = jnp.concatenate([up, split], axis=1)
    up_copy = swap(1, up, up_pair, up_other)

    def scatter(part, copy, pair_send, pair_recv, send, recv):
        copy.wait_recv()
        finish.append(copy.wait_send)
        both = pair_send[core].astype(jnp.float32) + pair_recv[...].astype(jnp.float32)
        send[...] = both.astype(jnp.bfloat16)
        arrive = exchange(
            "dp", 7 + part, CHIP_PEERS, lambda to: send.at[to // 2], recv, dp // 2
        )
        recv[dp // 2] = send[dp // 2]
        return arrive

    gate_arrive = scatter(0, gate_copy, gate_pair, gate_other, gate_send, gate_recv)
    up_arrive = scatter(1, up_copy, up_pair, up_other, up_send, up_recv)
    gate_arrive()
    gate = jnp.sum(gate_recv[...].astype(jnp.float32), axis=0)
    up_arrive()
    up = jnp.sum(up_recv[...].astype(jnp.float32), axis=0)
    squares = up[:, units : units + 1] + up[:, units + 1 : units + 2]
    inv_rms = 1.0 / jnp.sqrt(squares / model + 1e-06)
    gate = gate * inv_rms
    up = up[:, :units] * inv_rms
    hidden = gate / (1.0 + jnp.exp(-gate)) * up
    hidden_rows[dp] = hidden.astype(jnp.bfloat16)

    arrive = exchange("dp", 3, DP_PEERS, lambda to: hidden_rows.at[dp], hidden_rows, dp)
    loads[5].wait()
    arrive()
    down = lax.dot_general(
        hidden_rows[...].reshape(groups * rows, units),
        down_held[...],
        NT,
        preferred_element_type=jnp.float32,
    )
    down_send[:, :, :columns] = down.astype(jnp.bfloat16).reshape(groups, rows, columns)

    arrive = exchange("tp", 4, TP_PEERS, lambda to: down_send.at[to], down_recv, tp)
    down_recv[tp] = down_send[tp]
    arrive()
    result = jnp.sum(down_recv[:, :, :columns].astype(jnp.float32), axis=0)
    mixed[...] = (own.astype(jnp.float32) + result).astype(jnp.bfloat16)
    for sent in finish:
        sent()


def layer(
    lengths,
    query,
    cache,
    w_uk,
    w_value,
    sums,
    stats,
    w_out,
    residual,
    gain,
    w_gate,
    w_up,
    w_down,
    groups,
    model,
):
    rows, heads, depth = cache.shape[0], w_uk.shape[0], cache.shape[1]
    columns, units = w_down.shape
    wide = -(-columns // 128) * 128
    vmem = pl.BlockSpec(memory_space=pltpu.VMEM)
    anywhere = pl.BlockSpec(memory_space=pl.ANY)
    blocks = lambda width: pltpu.VMEM((groups, rows, width), jnp.bfloat16)
    half = lambda width: pltpu.VMEM((groups // 2, rows, width), jnp.bfloat16)
    pair = lambda width: pltpu.VMEM((2, groups // 2, rows, width), jnp.bfloat16)
    return pl.pallas_call(
        functools.partial(layer_kernel, model),
        out_shape=jax.ShapeDtypeStruct((rows, columns), jnp.bfloat16),
        in_specs=[anywhere] * 13,
        out_specs=vmem,
        scratch_shapes=[
            pltpu.SMEM(lengths.shape, jnp.int32),
            pltpu.VMEM(query.shape, jnp.bfloat16),
            pltpu.VMEM((rows, depth, FIRST), jnp.bfloat16),
            pltpu.VMEM(w_uk.shape, jnp.bfloat16),
            pltpu.VMEM(w_value.shape, jnp.bfloat16),
            pltpu.VMEM(sums.shape, jnp.float32),
            pltpu.VMEM(stats.shape, jnp.float32),
            pltpu.VMEM((rows, heads, depth), jnp.float32),
            pltpu.VMEM((rows, heads, FIRST), jnp.float32),
            pltpu.VMEM((heads, rows, KVR), jnp.float32),
            pltpu.VMEM((rows, heads * VD), jnp.bfloat16),
            pltpu.VMEM(w_out.shape, jnp.bfloat16),
            pltpu.VMEM(w_gate.shape, jnp.bfloat16),
            pltpu.VMEM(w_up.shape, jnp.bfloat16),
            pltpu.VMEM(w_down.shape, jnp.bfloat16),
            pltpu.VMEM(residual.shape, jnp.bfloat16),
            pltpu.VMEM(gain.shape, jnp.bfloat16),
            pltpu.VMEM(residual.shape[::-1], jnp.float32),
            blocks(heads * VD),
            blocks(wide),
            blocks(wide),
            blocks(wide),
            pair(units),
            half(units),
            half(units),
            half(units),
            pair(units + 128),
            half(units + 128),
            half(units + 128),
            half(units + 128),
            blocks(units),
            blocks(wide),
            blocks(wide),
            pltpu.SemaphoreType.DMA((6,)),
            pltpu.SemaphoreType.DMA((rows,)),
            pltpu.SemaphoreType.DMA((6,)),
            pltpu.SemaphoreType.DMA((9,)),
            pltpu.SemaphoreType.DMA((9,)),
        ],
        compiler_params=pltpu.CompilerParams(
            collective_id=0, has_side_effects=True, vmem_limit_bytes=VMEM_BYTES
        ),
        name="layer",
    )(
        lengths,
        query,
        cache,
        w_uk,
        w_value,
        sums,
        stats,
        w_out,
        residual,
        gain,
        w_gate,
        w_up,
        w_down,
    )


def solution(mesh):
    groups = mesh.shape["dp"]

    def on_device(
        query,
        latent_cache,
        lengths,
        w_uk,
        value_up_weight,
        w_out,
        residual,
        mlp_norm_scale,
        w_gate,
        w_up,
        w_down,
    ):
        cache = jnp.swapaxes(latent_cache, 1, 2)
        sums, stats = attend_later(query, cache, lengths, w_uk)
        return layer(
            lengths,
            query,
            cache,
            w_uk,
            value_up_weight,
            sums,
            stats,
            w_out.T,
            residual.T,
            mlp_norm_scale,
            w_gate,
            w_up,
            w_down.T,
            groups,
            groups * mlp_norm_scale.shape[0],
        )

    return jax.shard_map(
        on_device,
        mesh=mesh,
        in_specs=(
            P("dp", "tp"),
            P("dp", None, None),
            P("dp"),
            P("tp", None, None),
            P("tp", None, None),
            P("tp", "dp"),
            P(None, "dp"),
            P("dp"),
            P("dp", "tp"),
            P("dp", "tp"),
            P("tp", "dp"),
        ),
        out_specs=P("tp", "dp"),
        check_vma=False,
    )
```

```python
import functools

import jax
import jax.numpy as jnp
from jax import lax
from jax.experimental import pallas as pl
from jax.experimental.pallas import tpu as pltpu
from jax.sharding import PartitionSpec as P

CHIP_PEERS = sorted(
    [(a, b, 0) for a in range(2) for b in range(4) if a + b],
    key=lambda d: -(2 * d[0] + min(d[1], 4 - d[1])),
)
DP_PEERS = CHIP_PEERS + [(0, 0, 1)]
TP_PEERS = sorted(
    [(a, b) for a in range(8) for b in range(2) if a + b],
    key=lambda d: -(min(d[0], 8 - d[0]) + d[1]),
)
MESH = pl.DeviceIdType.MESH
NOPE = 128
ROPE = 64
KVR = 512
VD = 128
FIRST = 512
VMEM_BYTES = 60 * 2**20
NT = (((1,), (1,)), ((), ()))


def project(query, w_uk, queries):
    width = NOPE + ROPE
    for h in range(w_uk.shape[0]):
        nope = query[:, h * width : h * width + NOPE]
        queries[:, h, :KVR] = jnp.dot(nope, w_uk[h], preferred_element_type=jnp.float32)
        queries[:, h, KVR:] = query[:, h * width + NOPE : (h + 1) * width].astype(jnp.float32)


def live_scores(query, keys, first, length):
    got = jnp.dot(query, keys, preferred_element_type=jnp.float32)
    at = first + lax.broadcasted_iota(jnp.int32, got.shape, 1)
    return jnp.where(at < length, got * (1.0 / jnp.sqrt(jnp.float32(NOPE + ROPE))), -jnp.inf)


def weighted(probs, keys):
    return lax.dot_general(
        probs.astype(jnp.bfloat16), keys, NT, preferred_element_type=jnp.float32
    )


def later_kernel(
    lengths_in,
    query_in,
    cache,
    w_uk,
    queries,
    sums,
    stats,
    lengths,
    query,
    held,
    uk_held,
    wide_queries,
    cache_sem,
    load_sem,
):
    requests = queries.shape[0]
    most = cache.shape[2] // FIRST - 1
    loads = [
        pltpu.make_async_copy(src, dst, load_sem.at[at])
        for at, (src, dst) in enumerate(
            [(lengths_in, lengths), (w_uk, uk_held), (query_in, query)]
        )
    ]
    for load in loads:
        load.start()
    sums[...] = jnp.zeros_like(sums)
    stats[0] = jnp.full(stats.shape[1:], -1e30, jnp.float32)
    stats[1] = jnp.zeros(stats.shape[1:], jnp.float32)
    loads[0].wait()

    def each(step):
        @pl.loop(0, requests)
        def _(b):
            chunks = lax.div(lengths[b] - 1, FIRST)
            for k in range(1, most + 1):
                pl.when(chunks == k)(lambda k=k: step(b, k * FIRST))

    def copy(b, width):
        return pltpu.make_async_copy(
            cache.at[b, :, FIRST : FIRST + width], held.at[b, :, :width], cache_sem.at[b]
        )

    each(lambda b, width: copy(b, width).start())
    loads[1].wait()
    loads[2].wait()
    project(query, uk_held, wide_queries)
    queries[...] = wide_queries[...].astype(jnp.bfloat16)
    longest = lengths[0]
    for b in range(1, requests):
        longest = jnp.maximum(longest, lengths[b])

    @pl.when(longest > FIRST)
    def _():
        def step(b, width):
            copy(b, width).wait()
            scores = live_scores(queries[b], held[b, :, :width], FIRST, lengths[b])
            top = jnp.max(scores, axis=1, keepdims=True)
            probs = jnp.exp(scores - top)
            total = jnp.sum(probs, axis=1, keepdims=True)
            sums[b] = weighted(probs, held[b, :KVR, :width])
            stats[0, b] = jnp.broadcast_to(top, stats.shape[2:])
            stats[1, b] = jnp.broadcast_to(total, stats.shape[2:])

        each(step)


def attend_later(query, cache, lengths, w_uk):
    requests, depth, slots = cache.shape
    heads = w_uk.shape[0]
    vmem = pl.BlockSpec(memory_space=pltpu.VMEM)
    anywhere = pl.BlockSpec(memory_space=pl.ANY)
    return pl.pallas_call(
        later_kernel,
        out_shape=[
            jax.ShapeDtypeStruct((requests, heads, depth), jnp.bfloat16),
            jax.ShapeDtypeStruct((requests, heads, KVR), jnp.float32),
            jax.ShapeDtypeStruct((2, requests, heads, 128), jnp.float32),
        ],
        in_specs=[anywhere] * 4,
        out_specs=[vmem] * 3,
        scratch_shapes=[
            pltpu.SMEM(lengths.shape, jnp.int32),
            pltpu.VMEM(query.shape, jnp.bfloat16),
            pltpu.VMEM((requests, depth, slots - FIRST), jnp.bfloat16),
            pltpu.VMEM(w_uk.shape, jnp.bfloat16),
            pltpu.VMEM((requests, heads, depth), jnp.float32),
            pltpu.SemaphoreType.DMA((requests,)),
            pltpu.SemaphoreType.DMA((3,)),
        ],
        compiler_params=pltpu.CompilerParams(vmem_limit_bytes=VMEM_BYTES),
        name="attend_later",
    )(lengths, query, cache, w_uk)


def layer_kernel(
    model,
    lengths_in,
    cache,
    w_value,
    queries_in,
    sums_in,
    stats_in,
    w_out,
    residual,
    gain_in,
    w_gate,
    w_up,
    w_down,
    mixed,
    lengths,
    held,
    value_held,
    queries,
    sums,
    stats,
    context,
    values,
    out_held,
    gate_held,
    up_held,
    down_held,
    residual_held,
    gain,
    residual_rows,
    all_values,
    out_send,
    out_recv,
    stream_rows,
    gate_pair,
    gate_other,
    gate_send,
    gate_recv,
    up_pair,
    up_other,
    up_send,
    up_recv,
    hidden_block,
    hidden_rows,
    down_send,
    down_recv,
    attend_sem,
    cache_sem,
    weight_sem,
    send_sem,
    recv_sem,
):
    dp, tp = lax.axis_index("dp"), lax.axis_index("tp")
    groups = 2 * all_values.shape[1]
    rows = values.shape[0]
    columns = mixed.shape[1]
    units = gate_held.shape[1]

    requests = cache.shape[0]
    attend_loads = [
        pltpu.make_async_copy(src, dst, attend_sem.at[at])
        for at, (src, dst) in enumerate(
            [
                (queries_in, queries),
                (lengths_in, lengths),
                (stats_in, stats),
                (sums_in, sums),
                (w_value, value_held),
            ]
        )
    ]
    cache_loads = [
        pltpu.make_async_copy(cache.at[b, :, :FIRST], held.at[b], cache_sem.at[b])
        for b in range(requests)
    ]
    loads = [
        pltpu.make_async_copy(src, dst, weight_sem.at[at])
        for at, (src, dst) in enumerate(
            [
                (w_out, out_held),
                (residual, residual_held),
                (gain_in, gain),
                (w_gate, gate_held),
                (w_up, up_held),
                (w_down, down_held),
            ]
        )
    ]
    for load in attend_loads[:4] + cache_loads + attend_loads[4:] + loads:
        load.start()

    chip = dp // 2
    core, y, x_hi = lax.rem(dp, 2), lax.rem(dp // 2, 4), dp // 8
    x_lo, z = lax.rem(tp, 2), tp // 2

    def peer(axis, d):
        if axis == "dp":
            return (
                lax.rem(x_hi + d[0], 2) * 8 + lax.rem(y + d[1], 4) * 2 + lax.rem(core + d[2], 2)
            )
        return lax.rem(z + d[0], 8) * 2 + lax.rem(x_lo + d[1], 2)

    barrier = pltpu.get_barrier_semaphore()
    for axis, peers in (("dp", DP_PEERS), ("tp", TP_PEERS)):
        for d in peers:
            pl.semaphore_signal(
                barrier, inc=1, device_id={axis: peer(axis, d)}, device_id_type=MESH
            )

    for load in attend_loads[:4]:
        load.wait()

    def finish_request(b, scores):
        later = stats[0, b, :, :1]
        top = jnp.maximum(jnp.max(scores, axis=1, keepdims=True), later)
        share = jnp.exp(later - top)
        probs = jnp.exp(scores - top)
        total = jnp.sum(probs, axis=1, keepdims=True) + stats[1, b, :, :1] * share
        context[:, b, :] = (weighted(probs, held[b, :KVR, :]) + sums[b] * share) / total

    before = None
    for b in range(requests):
        cache_loads[b].wait()
        scores = live_scores(queries[b], held[b], 0, lengths[b])
        if b:
            finish_request(b - 1, before)
        before = scores
    finish_request(requests - 1, before)
    attend_loads[4].wait()
    for h in range(value_held.shape[0]):
        values[:, h * VD : (h + 1) * VD] = jnp.dot(
            context[h].astype(jnp.bfloat16), value_held[h], preferred_element_type=jnp.float32
        ).astype(jnp.bfloat16)

    pl.semaphore_wait(barrier, len(DP_PEERS) + len(TP_PEERS))
    finish = []

    def by_chip(blocks, wide):
        wide = wide.astype(jnp.bfloat16).reshape(2, groups // 2, rows, columns)
        blocks[:, 0, :, :columns] = wide[0]
        blocks[:, 1, :, :columns] = wide[1]

    def exchange(axis, phase, peers, source, target, place):
        for d in peers:
            to = peer(axis, d)
            pltpu.make_async_remote_copy(
                src_ref=source(to),
                dst_ref=target.at[place],
                send_sem=send_sem.at[phase],
                recv_sem=recv_sem.at[phase],
                device_id={axis: to},
                device_id_type=MESH,
            ).start()
        blocks = target.at[: len(peers)]
        finish.append(pltpu.make_async_copy(blocks, blocks, send_sem.at[phase]).wait)
        return pltpu.make_async_copy(blocks, blocks, recv_sem.at[phase]).wait

    other_core = {"dp": peer("dp", (0, 0, 1))}

    def gather(phase, block, target):
        arrive = exchange("dp", phase, CHIP_PEERS, lambda to: block, target.at[core], chip)
        target[core, chip] = block[...]

        def finished():
            arrive()
            copy = pltpu.make_async_remote_copy(
                src_ref=target.at[core],
                dst_ref=target.at[core],
                send_sem=send_sem.at[phase + 9],
                recv_sem=recv_sem.at[phase + 9],
                device_id=other_core,
                device_id_type=MESH,
            )
            copy.start()
            finish.append(copy.wait_send)
            theirs = target.at[1 - core]
            pltpu.make_async_copy(theirs, theirs, recv_sem.at[phase + 9]).wait()

        return finished

    arrive = gather(0, values, all_values)
    loads[1].wait()
    residual_rows[...] = residual_held[...].astype(jnp.float32).T
    loads[0].wait()
    arrive()
    attended = lax.dot_general(
        all_values[...].reshape(groups * rows, -1),
        out_held[...],
        NT,
        preferred_element_type=jnp.float32,
    )
    by_chip(out_send, attended)

    arrive = exchange(
        "tp", 2, TP_PEERS, lambda to: out_send.at[to // 2, lax.rem(to, 2)], out_recv, tp
    )
    out_recv[tp] = out_send[tp // 2, x_lo]
    arrive()
    own = residual_rows[pl.ds(pl.multiple_of(tp * rows, rows), rows), :]
    own = own + jnp.sum(out_recv[:, :, :columns].astype(jnp.float32), axis=0)
    own = own.astype(jnp.bfloat16)
    stream_rows[tp, :, :columns] = own

    arrive = exchange("tp", 3, TP_PEERS, lambda to: stream_rows.at[tp], stream_rows, tp)
    loads[2].wait()
    loads[3].wait()
    loads[4].wait()
    arrive()
    stream = stream_rows[:, :, :columns].astype(jnp.float32).reshape(groups * rows, columns)
    squares = jnp.sum(stream * stream, axis=1, keepdims=True)
    scaled = (stream * gain[...].astype(jnp.float32)[None, :]).astype(jnp.bfloat16)
    high = squares.astype(jnp.bfloat16).astype(jnp.float32)
    lane = lax.broadcasted_iota(jnp.int32, (groups * rows, 128), 1)
    split = jnp.where(lane == 0, high, jnp.where(lane == 1, squares - high, 0.0))

    def swap(part, wide, pair_send, pair_recv):
        chips = groups // 2
        blocks = wide.astype(jnp.bfloat16).reshape(chips, 2, rows, -1)
        pair_send[0] = blocks[:, 0]
        pair_send[1] = blocks[:, 1]
        copy = pltpu.make_async_remote_copy(
            src_ref=pair_send.at[1 - core],
            dst_ref=pair_recv,
            send_sem=send_sem.at[5 + part],
            recv_sem=recv_sem.at[5 + part],
            device_id=other_core,
            device_id_type=MESH,
        )
        copy.start()
        return copy

    gate = jnp.dot(scaled, gate_held[...], preferred_element_type=jnp.float32)
    gate_copy = swap(0, gate, gate_pair, gate_other)
    up = jnp.dot(scaled, up_held[...], preferred_element_type=jnp.float32)
    up = jnp.concatenate([up, split], axis=1)
    up_copy = swap(1, up, up_pair, up_other)

    def scatter(part, copy, pair_send, pair_recv, send, recv):
        copy.wait_recv()
        finish.append(copy.wait_send)
        both = pair_send[core].astype(jnp.float32) + pair_recv[...].astype(jnp.float32)
        send[...] = both.astype(jnp.bfloat16)
        arrive = exchange(
            "dp", 7 + part, CHIP_PEERS, lambda to: send.at[to // 2], recv, chip
        )
        recv[chip] = send[chip]
        return arrive

    gate_arrive = scatter(0, gate_copy, gate_pair, gate_other, gate_send, gate_recv)
    up_arrive = scatter(1, up_copy, up_pair, up_other, up_send, up_recv)
    gate_arrive()
    gate = jnp.sum(gate_recv[...].astype(jnp.float32), axis=0)
    up_arrive()
    up = jnp.sum(up_recv[...].astype(jnp.float32), axis=0)
    squares = up[:, units : units + 1] + up[:, units + 1 : units + 2]
    inv_rms = 1.0 / jnp.sqrt(squares / model + 1e-06)
    gate = gate * inv_rms
    up = up[:, :units] * inv_rms
    hidden = gate / (1.0 + jnp.exp(-gate)) * up
    hidden_block[...] = hidden.astype(jnp.bfloat16)

    arrive = gather(1, hidden_block, hidden_rows)
    loads[5].wait()
    arrive()
    down = lax.dot_general(
        hidden_rows[...].reshape(groups * rows, units),
        down_held[...],
        NT,
        preferred_element_type=jnp.float32,
    )
    by_chip(down_send, down)

    arrive = exchange(
        "tp", 4, TP_PEERS, lambda to: down_send.at[to // 2, lax.rem(to, 2)], down_recv, tp
    )
    down_recv[tp] = down_send[tp // 2, x_lo]
    arrive()
    result = jnp.sum(down_recv[:, :, :columns].astype(jnp.float32), axis=0)
    mixed[...] = (own.astype(jnp.float32) + result).astype(jnp.bfloat16)
    for sent in finish:
        sent()


def layer(
    lengths,
    cache,
    w_value,
    queries,
    sums,
    stats,
    w_out,
    residual,
    gain,
    w_gate,
    w_up,
    w_down,
    groups,
    model,
):
    rows, heads, depth = queries.shape
    columns, units = w_down.shape
    wide = -(-columns // 128) * 128
    vmem = pl.BlockSpec(memory_space=pltpu.VMEM)
    anywhere = pl.BlockSpec(memory_space=pl.ANY)
    blocks = lambda width: pltpu.VMEM((groups, rows, width), jnp.bfloat16)
    chips = lambda width: pltpu.VMEM((groups // 2, 2, rows, width), jnp.bfloat16)
    half = lambda width: pltpu.VMEM((groups // 2, rows, width), jnp.bfloat16)
    pair = lambda width: pltpu.VMEM((2, groups // 2, rows, width), jnp.bfloat16)
    return pl.pallas_call(
        functools.partial(layer_kernel, model),
        out_shape=jax.ShapeDtypeStruct((rows, columns), jnp.bfloat16),
        in_specs=[anywhere] * 12,
        out_specs=vmem,
        scratch_shapes=[
            pltpu.SMEM(lengths.shape, jnp.int32),
            pltpu.VMEM((rows, depth, FIRST), jnp.bfloat16),
            pltpu.VMEM(w_value.shape, jnp.bfloat16),
            pltpu.VMEM(queries.shape, jnp.bfloat16),
            pltpu.VMEM(sums.shape, jnp.float32),
            pltpu.VMEM(stats.shape, jnp.float32),
            pltpu.VMEM((heads, rows, KVR), jnp.float32),
            pltpu.VMEM((rows, heads * VD), jnp.bfloat16),
            pltpu.VMEM(w_out.shape, jnp.bfloat16),
            pltpu.VMEM(w_gate.shape, jnp.bfloat16),
            pltpu.VMEM(w_up.shape, jnp.bfloat16),
            pltpu.VMEM(w_down.shape, jnp.bfloat16),
            pltpu.VMEM(residual.shape, jnp.bfloat16),
            pltpu.VMEM(gain.shape, jnp.bfloat16),
            pltpu.VMEM(residual.shape[::-1], jnp.float32),
            pair(heads * VD),
            chips(wide),
            blocks(wide),
            blocks(wide),
            pair(units),
            half(units),
            half(units),
            half(units),
            pair(units + 128),
            half(units + 128),
            half(units + 128),
            half(units + 128),
            pltpu.VMEM((rows, units), jnp.bfloat16),
            pair(units),
            chips(wide),
            blocks(wide),
            pltpu.SemaphoreType.DMA((5,)),
            pltpu.SemaphoreType.DMA((rows,)),
            pltpu.SemaphoreType.DMA((6,)),
            pltpu.SemaphoreType.DMA((11,)),
            pltpu.SemaphoreType.DMA((11,)),
        ],
        compiler_params=pltpu.CompilerParams(
            collective_id=0, has_side_effects=True, vmem_limit_bytes=VMEM_BYTES
        ),
        name="layer",
    )(
        lengths,
        cache,
        w_value,
        queries,
        sums,
        stats,
        w_out,
        residual,
        gain,
        w_gate,
        w_up,
        w_down,
    )


def solution(mesh):
    groups = mesh.shape["dp"]

    def on_device(
        query,
        latent_cache,
        lengths,
        w_uk,
        value_up_weight,
        w_out,
        residual,
        mlp_norm_scale,
        w_gate,
        w_up,
        w_down,
    ):
        cache = jnp.swapaxes(latent_cache, 1, 2)
        queries, sums, stats = attend_later(query, cache, lengths, w_uk)
        return layer(
            lengths,
            cache,
            value_up_weight,
            queries,
            sums,
            stats,
            w_out.T,
            residual.T,
            mlp_norm_scale,
            w_gate,
            w_up,
            w_down.T,
            groups,
            groups * mlp_norm_scale.shape[0],
        )

    return jax.shard_map(
        on_device,
        mesh=mesh,
        in_specs=(
            P("dp", "tp"),
            P("dp", None, None),
            P("dp"),
            P("tp", None, None),
            P("tp", None, None),
            P("tp", "dp"),
            P(None, "dp"),
            P("dp"),
            P("dp", "tp"),
            P("dp", "tp"),
            P("tp", "dp"),
        ),
        out_specs=P("tp", "dp"),
        check_vma=False,
    )
```

```python
import functools

import jax
import jax.numpy as jnp
from jax import lax
from jax.experimental import pallas as pl
from jax.experimental.pallas import tpu as pltpu
from jax.sharding import PartitionSpec as P

DP_PEERS = sorted(
    [(a, b, c) for a in range(2) for b in range(4) for c in range(2) if a + b + c],
    key=lambda d: -(2 * d[0] + min(d[1], 4 - d[1])),
)
CHIP_PEERS = [d for d in DP_PEERS if d[2] == 0]
TP_PEERS = sorted(
    [(a, b) for a in range(8) for b in range(2) if a + b],
    key=lambda d: -(min(d[0], 8 - d[0]) + d[1]),
)
MESH = pl.DeviceIdType.MESH
NOPE = 128
ROPE = 64
KVR = 512
VD = 128
FIRST = 512
TOGETHER = 4
VMEM_BYTES = 60 * 2**20
NT = (((1,), (1,)), ((), ()))


def project(query, w_uk, queries):
    width = NOPE + ROPE
    for h in range(w_uk.shape[0]):
        nope = query[:, h * width : h * width + NOPE]
        queries[:, h, :KVR] = jnp.dot(nope, w_uk[h], preferred_element_type=jnp.float32)
        queries[:, h, KVR:] = query[:, h * width + NOPE : (h + 1) * width].astype(jnp.float32)


def live_scores(query, keys, first, length):
    got = jnp.dot(query, keys, preferred_element_type=jnp.float32)
    at = first + lax.broadcasted_iota(jnp.int32, got.shape, 1)
    return jnp.where(at < length, got * (1.0 / jnp.sqrt(jnp.float32(NOPE + ROPE))), -jnp.inf)


def weighted(probs, keys):
    return lax.dot_general(
        probs.astype(jnp.bfloat16), keys, NT, preferred_element_type=jnp.float32
    )


def later_kernel(
    lengths_in,
    query_in,
    cache,
    w_uk,
    queries,
    sums,
    stats,
    lengths,
    query,
    held,
    uk_held,
    wide_queries,
    cache_sem,
    load_sem,
):
    requests = queries.shape[0]
    most = cache.shape[2] // FIRST - 1
    loads = [
        pltpu.make_async_copy(src, dst, load_sem.at[at])
        for at, (src, dst) in enumerate(
            [(lengths_in, lengths), (w_uk, uk_held), (query_in, query)]
        )
    ]
    for load in loads:
        load.start()
    sums[...] = jnp.zeros_like(sums)
    stats[0] = jnp.full(stats.shape[1:], -1e30, jnp.float32)
    stats[1] = jnp.zeros(stats.shape[1:], jnp.float32)
    loads[0].wait()

    def each(step):
        @pl.loop(0, requests)
        def _(b):
            chunks = lax.div(lengths[b] - 1, FIRST)
            for k in range(1, most + 1):
                pl.when(chunks == k)(lambda k=k: step(b, k * FIRST))

    def copy(b, width):
        return pltpu.make_async_copy(
            cache.at[b, :, FIRST : FIRST + width], held.at[b, :, :width], cache_sem.at[b]
        )

    each(lambda b, width: copy(b, width).start())
    loads[1].wait()
    loads[2].wait()
    project(query, uk_held, wide_queries)
    queries[...] = wide_queries[...].astype(jnp.bfloat16)
    longest = lengths[0]
    for b in range(1, requests):
        longest = jnp.maximum(longest, lengths[b])

    @pl.when(longest > FIRST)
    def _():
        def step(b, width):
            copy(b, width).wait()
            scores = live_scores(queries[b], held[b, :, :width], FIRST, lengths[b])
            top = jnp.max(scores, axis=1, keepdims=True)
            probs = jnp.exp(scores - top)
            total = jnp.sum(probs, axis=1, keepdims=True)
            sums[b] = weighted(probs, held[b, :KVR, :width])
            stats[0, b] = jnp.broadcast_to(top, stats.shape[2:])
            stats[1, b] = jnp.broadcast_to(total, stats.shape[2:])

        each(step)


def attend_later(query, cache, lengths, w_uk):
    requests, depth, slots = cache.shape
    heads = w_uk.shape[0]
    vmem = pl.BlockSpec(memory_space=pltpu.VMEM)
    anywhere = pl.BlockSpec(memory_space=pl.ANY)
    return pl.pallas_call(
        later_kernel,
        out_shape=[
            jax.ShapeDtypeStruct((requests, heads, depth), jnp.bfloat16),
            jax.ShapeDtypeStruct((requests, heads, KVR), jnp.float32),
            jax.ShapeDtypeStruct((2, requests, heads, 128), jnp.float32),
        ],
        in_specs=[anywhere] * 4,
        out_specs=[vmem] * 3,
        scratch_shapes=[
            pltpu.SMEM(lengths.shape, jnp.int32),
            pltpu.VMEM(query.shape, jnp.bfloat16),
            pltpu.VMEM((requests, depth, slots - FIRST), jnp.bfloat16),
            pltpu.VMEM(w_uk.shape, jnp.bfloat16),
            pltpu.VMEM((requests, heads, depth), jnp.float32),
            pltpu.SemaphoreType.DMA((requests,)),
            pltpu.SemaphoreType.DMA((3,)),
        ],
        compiler_params=pltpu.CompilerParams(vmem_limit_bytes=VMEM_BYTES),
        name="attend_later",
    )(lengths, query, cache, w_uk)


def layer_kernel(
    model,
    lengths_in,
    cache,
    w_value,
    queries_in,
    sums_in,
    stats_in,
    w_out,
    residual,
    gain_in,
    w_gate,
    w_up,
    w_down,
    mixed,
    lengths,
    held,
    value_held,
    queries,
    sums,
    stats,
    context,
    values,
    out_held,
    gate_held,
    up_held,
    down_held,
    residual_held,
    gain,
    residual_rows,
    all_values,
    out_send,
    out_recv,
    stream_rows,
    gate_pair,
    gate_other,
    gate_send,
    gate_recv,
    up_pair,
    up_other,
    up_send,
    up_recv,
    hidden_block,
    hidden_rows,
    down_send,
    down_recv,
    attend_sem,
    cache_sem,
    weight_sem,
    send_sem,
    recv_sem,
):
    dp, tp = lax.axis_index("dp"), lax.axis_index("tp")
    groups = all_values.shape[0]
    rows = values.shape[0]
    columns = mixed.shape[1]
    units = gate_held.shape[1]

    requests = cache.shape[0]
    attend_loads = [
        pltpu.make_async_copy(src, dst, attend_sem.at[at])
        for at, (src, dst) in enumerate(
            [
                (queries_in, queries),
                (lengths_in, lengths),
                (stats_in, stats),
                (sums_in, sums),
                (w_value, value_held),
            ]
        )
    ]
    cache_loads = [
        pltpu.make_async_copy(cache.at[b, :, :FIRST], held.at[b], cache_sem.at[b])
        for b in range(requests)
    ]
    loads = [
        pltpu.make_async_copy(src, dst, weight_sem.at[at])
        for at, (src, dst) in enumerate(
            [
                (w_out, out_held),
                (residual, residual_held),
                (gain_in, gain),
                (w_gate, gate_held),
                (w_up, up_held),
                (w_down, down_held),
            ]
        )
    ]
    for load in attend_loads[:4] + cache_loads + attend_loads[4:] + loads:
        load.start()

    chip = dp // 2
    core, y, x_hi = lax.rem(dp, 2), lax.rem(dp // 2, 4), dp // 8
    x_lo, z = lax.rem(tp, 2), tp // 2

    def peer(axis, d):
        if axis == "dp":
            return (
                lax.rem(x_hi + d[0], 2) * 8 + lax.rem(y + d[1], 4) * 2 + lax.rem(core + d[2], 2)
            )
        return lax.rem(z + d[0], 8) * 2 + lax.rem(x_lo + d[1], 2)

    barrier = pltpu.get_barrier_semaphore()
    for axis, peers in (("dp", DP_PEERS), ("tp", TP_PEERS)):
        for d in peers:
            pl.semaphore_signal(
                barrier, inc=1, device_id={axis: peer(axis, d)}, device_id_type=MESH
            )

    for load in attend_loads[:4]:
        load.wait()

    def finish_request(b, scores):
        later = stats[0, b, :, :1]
        top = jnp.maximum(jnp.max(scores, axis=1, keepdims=True), later)
        share = jnp.exp(later - top)
        probs = jnp.exp(scores - top)
        total = jnp.sum(probs, axis=1, keepdims=True) + stats[1, b, :, :1] * share
        context[:, b, :] = (weighted(probs, held[b, :KVR, :]) + sums[b] * share) * (1.0 / total)

    before = []
    for first in range(0, requests, TOGETHER):
        some = range(first, first + TOGETHER)
        for b in some:
            cache_loads[b].wait()
        now = [(b, live_scores(queries[b], held[b], 0, lengths[b])) for b in some]
        for b, scores in before:
            finish_request(b, scores)
        before = now
    for b, scores in before:
        finish_request(b, scores)
    attend_loads[4].wait()
    for h in range(value_held.shape[0]):
        values[:, h * VD : (h + 1) * VD] = jnp.dot(
            context[h].astype(jnp.bfloat16), value_held[h], preferred_element_type=jnp.float32
        ).astype(jnp.bfloat16)

    pl.semaphore_wait(barrier, len(DP_PEERS) + len(TP_PEERS))
    finish = []

    def in_blocks(blocks, wide):
        blocks[:, :, :columns] = wide.astype(jnp.bfloat16).reshape(groups, rows, columns)

    def exchange(axis, phase, peers, source, target, place):
        for d in peers:
            to = peer(axis, d)
            pltpu.make_async_remote_copy(
                src_ref=source(to),
                dst_ref=target.at[place],
                send_sem=send_sem.at[phase],
                recv_sem=recv_sem.at[phase],
                device_id={axis: to},
                device_id_type=MESH,
            ).start()
        blocks = target.at[: len(peers)]
        finish.append(pltpu.make_async_copy(blocks, blocks, send_sem.at[phase]).wait)
        return pltpu.make_async_copy(blocks, blocks, recv_sem.at[phase]).wait

    other_core = {"dp": peer("dp", (0, 0, 1))}

    def gather(phase, block, target):
        arrive = exchange("dp", phase, DP_PEERS, lambda to: block, target, dp)
        target[dp] = block[...]
        return arrive

    arrive = gather(0, values, all_values)
    loads[1].wait()
    residual_rows[...] = residual_held[...].astype(jnp.float32).T
    loads[0].wait()
    arrive()
    attended = lax.dot_general(
        all_values[...].reshape(groups * rows, -1),
        out_held[...],
        NT,
        preferred_element_type=jnp.float32,
    )
    in_blocks(out_send, attended)

    arrive = exchange("tp", 2, TP_PEERS, lambda to: out_send.at[to], out_recv, tp)
    out_recv[tp] = out_send[tp]
    arrive()
    own = residual_rows[pl.ds(pl.multiple_of(tp * rows, rows), rows), :]
    own = own + jnp.sum(out_recv[:, :, :columns].astype(jnp.float32), axis=0)
    own = own.astype(jnp.bfloat16)
    stream_rows[tp, :, :columns] = own

    arrive = exchange("tp", 3, TP_PEERS, lambda to: stream_rows.at[tp], stream_rows, tp)
    loads[2].wait()
    loads[3].wait()
    loads[4].wait()
    arrive()
    stream = stream_rows[:, :, :columns].astype(jnp.float32).reshape(groups * rows, columns)
    squares = jnp.sum(stream * stream, axis=1, keepdims=True)
    scaled = (stream * gain[...].astype(jnp.float32)[None, :]).astype(jnp.bfloat16)
    high = squares.astype(jnp.bfloat16).astype(jnp.float32)
    lane = lax.broadcasted_iota(jnp.int32, (groups * rows, 128), 1)
    split = jnp.where(lane == 0, high, jnp.where(lane == 1, squares - high, 0.0))

    def swap(part, wide, pair_send, pair_recv):
        chips = groups // 2
        blocks = wide.astype(jnp.bfloat16).reshape(chips, 2, rows, -1)
        pair_send[0] = blocks[:, 0]
        pair_send[1] = blocks[:, 1]
        copy = pltpu.make_async_remote_copy(
            src_ref=pair_send.at[1 - core],
            dst_ref=pair_recv,
            send_sem=send_sem.at[5 + part],
            recv_sem=recv_sem.at[5 + part],
            device_id=other_core,
            device_id_type=MESH,
        )
        copy.start()
        return copy

    gate = jnp.dot(scaled, gate_held[...], preferred_element_type=jnp.float32)
    gate_copy = swap(0, gate, gate_pair, gate_other)
    up = jnp.dot(scaled, up_held[...], preferred_element_type=jnp.float32)
    up = jnp.concatenate([up, split], axis=1)
    up_copy = swap(1, up, up_pair, up_other)

    def scatter(part, copy, pair_send, pair_recv, send, recv):
        copy.wait_recv()
        finish.append(copy.wait_send)
        both = pair_send[core].astype(jnp.float32) + pair_recv[...].astype(jnp.float32)
        send[...] = both.astype(jnp.bfloat16)
        arrive = exchange(
            "dp", 7 + part, CHIP_PEERS, lambda to: send.at[to // 2], recv, chip
        )
        recv[chip] = send[chip]
        return arrive

    gate_arrive = scatter(0, gate_copy, gate_pair, gate_other, gate_send, gate_recv)
    up_arrive = scatter(1, up_copy, up_pair, up_other, up_send, up_recv)
    gate_arrive()
    gate = jnp.sum(gate_recv[...].astype(jnp.float32), axis=0)
    up_arrive()
    up = jnp.sum(up_recv[...].astype(jnp.float32), axis=0)
    squares = up[:, units : units + 1] + up[:, units + 1 : units + 2]
    inv_rms = 1.0 / jnp.sqrt(squares / model + 1e-06)
    gate = gate * inv_rms
    up = up[:, :units] * inv_rms
    hidden = gate / (1.0 + jnp.exp(-gate)) * up
    hidden_block[...] = hidden.astype(jnp.bfloat16)

    arrive = gather(1, hidden_block, hidden_rows)
    loads[5].wait()
    arrive()
    down = lax.dot_general(
        hidden_rows[...].reshape(groups * rows, units),
        down_held[...],
        NT,
        preferred_element_type=jnp.float32,
    )
    in_blocks(down_send, down)

    arrive = exchange("tp", 4, TP_PEERS, lambda to: down_send.at[to], down_recv, tp)
    down_recv[tp] = down_send[tp]
    arrive()
    result = jnp.sum(down_recv[:, :, :columns].astype(jnp.float32), axis=0)
    mixed[...] = (own.astype(jnp.float32) + result).astype(jnp.bfloat16)
    for sent in finish:
        sent()


def layer(
    lengths,
    cache,
    w_value,
    queries,
    sums,
    stats,
    w_out,
    residual,
    gain,
    w_gate,
    w_up,
    w_down,
    groups,
    model,
):
    rows, heads, depth = queries.shape
    columns, units = w_down.shape
    wide = -(-columns // 128) * 128
    vmem = pl.BlockSpec(memory_space=pltpu.VMEM)
    anywhere = pl.BlockSpec(memory_space=pl.ANY)
    blocks = lambda width: pltpu.VMEM((groups, rows, width), jnp.bfloat16)
    half = lambda width: pltpu.VMEM((groups // 2, rows, width), jnp.bfloat16)
    pair = lambda width: pltpu.VMEM((2, groups // 2, rows, width), jnp.bfloat16)
    return pl.pallas_call(
        functools.partial(layer_kernel, model),
        out_shape=jax.ShapeDtypeStruct((rows, columns), jnp.bfloat16),
        in_specs=[anywhere] * 12,
        out_specs=vmem,
        scratch_shapes=[
            pltpu.SMEM(lengths.shape, jnp.int32),
            pltpu.VMEM((rows, depth, FIRST), jnp.bfloat16),
            pltpu.VMEM(w_value.shape, jnp.bfloat16),
            pltpu.VMEM(queries.shape, jnp.bfloat16),
            pltpu.VMEM(sums.shape, jnp.float32),
            pltpu.VMEM(stats.shape, jnp.float32),
            pltpu.VMEM((heads, rows, KVR), jnp.float32),
            pltpu.VMEM((rows, heads * VD), jnp.bfloat16),
            pltpu.VMEM(w_out.shape, jnp.bfloat16),
            pltpu.VMEM(w_gate.shape, jnp.bfloat16),
            pltpu.VMEM(w_up.shape, jnp.bfloat16),
            pltpu.VMEM(w_down.shape, jnp.bfloat16),
            pltpu.VMEM(residual.shape, jnp.bfloat16),
            pltpu.VMEM(gain.shape, jnp.bfloat16),
            pltpu.VMEM(residual.shape[::-1], jnp.float32),
            blocks(heads * VD),
            blocks(wide),
            blocks(wide),
            blocks(wide),
            pair(units),
            half(units),
            half(units),
            half(units),
            pair(units + 128),
            half(units + 128),
            half(units + 128),
            half(units + 128),
            pltpu.VMEM((rows, units), jnp.bfloat16),
            blocks(units),
            blocks(wide),
            blocks(wide),
            pltpu.SemaphoreType.DMA((5,)),
            pltpu.SemaphoreType.DMA((rows,)),
            pltpu.SemaphoreType.DMA((6,)),
            pltpu.SemaphoreType.DMA((9,)),
            pltpu.SemaphoreType.DMA((9,)),
        ],
        compiler_params=pltpu.CompilerParams(
            collective_id=0, has_side_effects=True, vmem_limit_bytes=VMEM_BYTES
        ),
        name="layer",
    )(
        lengths,
        cache,
        w_value,
        queries,
        sums,
        stats,
        w_out,
        residual,
        gain,
        w_gate,
        w_up,
        w_down,
    )


def solution(mesh):
    groups = mesh.shape["dp"]

    def on_device(
        query,
        latent_cache,
        lengths,
        w_uk,
        value_up_weight,
        w_out,
        residual,
        mlp_norm_scale,
        w_gate,
        w_up,
        w_down,
    ):
        cache = jnp.swapaxes(latent_cache, 1, 2)
        queries, sums, stats = attend_later(query, cache, lengths, w_uk)
        return layer(
            lengths,
            cache,
            value_up_weight,
            queries,
            sums,
            stats,
            w_out.T,
            residual.T,
            mlp_norm_scale,
            w_gate,
            w_up,
            w_down.T,
            groups,
            groups * mlp_norm_scale.shape[0],
        )

    return jax.shard_map(
        on_device,
        mesh=mesh,
        in_specs=(
            P("dp", "tp"),
            P("dp", None, None),
            P("dp"),
            P("tp", None, None),
            P("tp", None, None),
            P("tp", "dp"),
            P(None, "dp"),
            P("dp"),
            P("dp", "tp"),
            P("dp", "tp"),
            P("tp", "dp"),
        ),
        out_specs=P("tp", "dp"),
        check_vma=False,
    )
```

```python
import functools

import jax
import jax.numpy as jnp
from jax import lax
from jax.experimental import pallas as pl
from jax.experimental.pallas import tpu as pltpu
from jax.sharding import PartitionSpec as P

CHIP_PEERS = sorted(
    [(a, b) for a in range(2) for b in range(4) if a + b],
    key=lambda d: -(2 * d[0] + min(d[1], 4 - d[1])),
)
TP_PEERS = sorted(
    [(a, b) for a in range(8) for b in range(2) if a + b],
    key=lambda d: -(min(d[0], 8 - d[0]) + d[1]),
)
MESH = pl.DeviceIdType.MESH
NOPE = 128
ROPE = 64
KVR = 512
VD = 128
FIRST = 512
TOGETHER = 4
VMEM_BYTES = 60 * 2**20
NT = (((1,), (1,)), ((), ()))


def project(query, w_uk, queries):
    width = NOPE + ROPE
    for h in range(w_uk.shape[0]):
        nope = query[:, h * width : h * width + NOPE]
        queries[:, h, :KVR] = jnp.dot(nope, w_uk[h], preferred_element_type=jnp.float32)
        queries[:, h, KVR:] = query[:, h * width + NOPE : (h + 1) * width].astype(jnp.float32)


def live_scores(query, keys, first, length):
    got = jnp.dot(query, keys, preferred_element_type=jnp.float32)
    at = first + lax.broadcasted_iota(jnp.int32, got.shape, 1)
    return jnp.where(at < length, got * (1.0 / jnp.sqrt(jnp.float32(NOPE + ROPE))), -jnp.inf)


def weighted(probs, keys):
    return lax.dot_general(
        probs.astype(jnp.bfloat16), keys, NT, preferred_element_type=jnp.float32
    )


def later_kernel(
    lengths_in,
    query_in,
    cache,
    w_uk,
    queries,
    sums,
    stats,
    lengths,
    query,
    held,
    uk_held,
    wide_queries,
    cache_sem,
    load_sem,
):
    requests = queries.shape[0]
    most = cache.shape[2] // FIRST - 1
    loads = [
        pltpu.make_async_copy(src, dst, load_sem.at[at])
        for at, (src, dst) in enumerate(
            [(lengths_in, lengths), (w_uk, uk_held), (query_in, query)]
        )
    ]
    for load in loads:
        load.start()
    sums[...] = jnp.zeros_like(sums)
    stats[0] = jnp.full(stats.shape[1:], -1e30, jnp.float32)
    stats[1] = jnp.zeros(stats.shape[1:], jnp.float32)
    loads[0].wait()

    def each(step):
        @pl.loop(0, requests)
        def _(b):
            chunks = lax.div(lengths[b] - 1, FIRST)
            for k in range(1, most + 1):
                pl.when(chunks == k)(lambda k=k: step(b, k * FIRST))

    def copy(b, width):
        return pltpu.make_async_copy(
            cache.at[b, :, FIRST : FIRST + width], held.at[b, :, :width], cache_sem.at[b]
        )

    each(lambda b, width: copy(b, width).start())
    loads[1].wait()
    loads[2].wait()
    project(query, uk_held, wide_queries)
    queries[...] = wide_queries[...].astype(jnp.bfloat16)
    longest = lengths[0]
    for b in range(1, requests):
        longest = jnp.maximum(longest, lengths[b])

    @pl.when(longest > FIRST)
    def _():
        def step(b, width):
            copy(b, width).wait()
            scores = live_scores(queries[b], held[b, :, :width], FIRST, lengths[b])
            top = jnp.max(scores, axis=1, keepdims=True)
            probs = jnp.exp(scores - top)
            total = jnp.sum(probs, axis=1, keepdims=True)
            sums[b] = weighted(probs, held[b, :KVR, :width])
            stats[0, b] = jnp.broadcast_to(top, stats.shape[2:])
            stats[1, b] = jnp.broadcast_to(total, stats.shape[2:])

        each(step)


def attend_later(query, cache, lengths, w_uk):
    requests, depth, slots = cache.shape
    heads = w_uk.shape[0]
    vmem = pl.BlockSpec(memory_space=pltpu.VMEM)
    anywhere = pl.BlockSpec(memory_space=pl.ANY)
    return pl.pallas_call(
        later_kernel,
        out_shape=[
            jax.ShapeDtypeStruct((requests, heads, depth), jnp.bfloat16),
            jax.ShapeDtypeStruct((requests, heads, KVR), jnp.float32),
            jax.ShapeDtypeStruct((2, requests, heads, 128), jnp.float32),
        ],
        in_specs=[anywhere] * 4,
        out_specs=[vmem] * 3,
        scratch_shapes=[
            pltpu.SMEM(lengths.shape, jnp.int32),
            pltpu.VMEM(query.shape, jnp.bfloat16),
            pltpu.VMEM((requests, depth, slots - FIRST), jnp.bfloat16),
            pltpu.VMEM(w_uk.shape, jnp.bfloat16),
            pltpu.VMEM((requests, heads, depth), jnp.float32),
            pltpu.SemaphoreType.DMA((requests,)),
            pltpu.SemaphoreType.DMA((3,)),
        ],
        compiler_params=pltpu.CompilerParams(vmem_limit_bytes=VMEM_BYTES),
        name="attend_later",
    )(lengths, query, cache, w_uk)


def layer_kernel(
    model,
    lengths_in,
    cache,
    w_value,
    queries_in,
    sums_in,
    stats_in,
    w_out,
    residual,
    gain_in,
    w_gate,
    w_up,
    w_down,
    mixed,
    lengths,
    held,
    value_held,
    queries,
    sums,
    stats,
    context,
    values,
    out_held,
    gate_held,
    up_held,
    down_held,
    residual_held,
    gain,
    residual_rows,
    all_values,
    out_send,
    out_recv,
    gains,
    stream_own,
    stream_rows,
    base,
    first_send,
    first_recv,
    second_send,
    second_recv,
    hidden_block,
    hidden_rows,
    rest_block,
    rest_rows,
    down_send,
    down_other,
    down_recv,
    attend_sem,
    cache_sem,
    weight_sem,
    send_sem,
    recv_sem,
):
    dp, tp = lax.axis_index("dp"), lax.axis_index("tp")
    groups = out_recv.shape[0]
    rows = values.shape[0]
    columns = mixed.shape[1]
    units = gate_held.shape[2]
    chips = groups // 2

    chip = dp // 2
    core, y, x_hi = lax.rem(dp, 2), lax.rem(dp // 2, 4), dp // 8
    x_lo, z = lax.rem(tp, 2), tp // 2
    requests = cache.shape[0]
    attend_loads = [
        pltpu.make_async_copy(src, dst, attend_sem.at[at])
        for at, (src, dst) in enumerate(
            [
                (queries_in, queries),
                (lengths_in, lengths),
                (stats_in, stats),
                (sums_in, sums),
                (w_value, value_held),
            ]
        )
    ]
    cache_loads = [
        pltpu.make_async_copy(cache.at[b, :, :FIRST], held.at[b], cache_sem.at[b])
        for b in range(requests)
    ]
    loads = [
        pltpu.make_async_copy(src, dst, weight_sem.at[at])
        for at, (src, dst) in enumerate(
            [
                (w_out, out_held.at[core]),
                (residual, residual_held.at[core]),
                (gain_in, gain),
                (w_gate, gate_held.at[core]),
                (w_up, up_held.at[core]),
                (w_down, down_held.at[core]),
            ]
        )
    ]
    for load in attend_loads[:4] + cache_loads + attend_loads[4:] + loads:
        load.start()

    def along(axis, d):
        if axis == "dp":
            return {"dp": lax.rem(x_hi + d[0], 2) * 8 + lax.rem(y + d[1], 4) * 2 + core}
        return {"tp": lax.rem(z + d[0], 8) * 2 + lax.rem(x_lo + d[1], 2)}

    other_dp = chip * 2 + 1 - core
    other_core = {"dp": other_dp, "tp": tp}
    barrier = pltpu.get_barrier_semaphore()
    partners = [along("dp", d) for d in CHIP_PEERS] + [along("tp", d) for d in TP_PEERS]
    partners.append(other_core)
    for partner in partners:
        pl.semaphore_signal(barrier, inc=1, device_id=partner, device_id_type=MESH)

    for load in attend_loads[:4]:
        load.wait()

    def finish_request(b, scores):
        later = stats[0, b, :, :1]
        top = jnp.maximum(jnp.max(scores, axis=1, keepdims=True), later)
        share = jnp.exp(later - top)
        probs = jnp.exp(scores - top)
        total = jnp.sum(probs, axis=1, keepdims=True) + stats[1, b, :, :1] * share
        context[:, b, :] = (weighted(probs, held[b, :KVR, :]) + sums[b] * share) * (1.0 / total)

    before = []
    for first in range(0, requests, TOGETHER):
        some = range(first, first + TOGETHER)
        for b in some:
            cache_loads[b].wait()
        now = [(b, live_scores(queries[b], held[b], 0, lengths[b])) for b in some]
        for b, scores in before:
            finish_request(b, scores)
        before = now
    for b, scores in before:
        finish_request(b, scores)
    attend_loads[4].wait()
    for h in range(value_held.shape[0]):
        values[:, h * VD : (h + 1) * VD] = jnp.dot(
            context[h].astype(jnp.bfloat16), value_held[h], preferred_element_type=jnp.float32
        ).astype(jnp.bfloat16)

    pl.semaphore_wait(barrier, len(partners))
    finish = []

    def send(block, place, device, phase):
        copy = pltpu.make_async_remote_copy(
            src_ref=block,
            dst_ref=place,
            send_sem=send_sem.at[phase],
            recv_sem=recv_sem.at[phase],
            device_id=device,
            device_id_type=MESH,
        )
        copy.start()
        return copy

    def exchange(axis, phase, source, target, place):
        peers = CHIP_PEERS if axis == "dp" else TP_PEERS
        for d in peers:
            to = along(axis, d)
            at = to["dp"] // 2 if axis == "dp" else to["tp"]
            send(source(at), target.at[place], to, phase)
        blocks = target.at[: len(peers)]
        finish.append(pltpu.make_async_copy(blocks, blocks, send_sem.at[phase]).wait)
        return pltpu.make_async_copy(blocks, blocks, recv_sem.at[phase]).wait

    def gather(phase, block, target):
        arrive = exchange("dp", phase, lambda to: block, target, chip)
        target[chip] = block[...]
        return arrive

    def swap(phase, source, held):
        finish.append(send(source, held.at[core], other_core, phase).wait_send)
        theirs = held.at[1 - core]
        return pltpu.make_async_copy(theirs, theirs, recv_sem.at[phase]).wait

    arrive = gather(0, values, all_values)
    loads[2].wait()
    own_gain = gain[...].astype(jnp.float32)[None, :]
    gains[core, :, :columns] = jnp.broadcast_to(own_gain, (rows, columns)).astype(jnp.bfloat16)
    out_swap = swap(9, w_out, out_held)
    residual_swap = swap(10, residual, residual_held)
    gain_swap = swap(11, gains.at[core], gains)
    gate_swap = swap(12, w_gate, gate_held)
    up_swap = swap(13, w_up, up_held)
    down_swap = swap(14, w_down, down_held)
    loads[1].wait()
    residual_swap()
    for side in range(2):
        residual_rows[side] = residual_held[side].astype(jnp.float32).T
    loads[0].wait()
    out_swap()
    arrive()
    every = all_values[...].reshape(chips * rows, -1)
    for side in range(2):
        attended = lax.dot_general(every, out_held[side], NT, preferred_element_type=jnp.float32)
        attended = attended.astype(jnp.bfloat16).reshape(chips, rows, columns)
        out_send[:, side, :, :columns] = attended

    arrive = exchange("tp", 3, lambda to: out_send.at[to // 2, lax.rem(to, 2)], out_recv, tp)
    out_recv[tp] = out_send[z, x_lo]
    arrive()
    own_rows = pl.ds(pl.multiple_of((2 * z + core) * rows, rows), rows)
    own = residual_rows[x_lo, own_rows, :]
    own = own + jnp.sum(out_recv[:, :, :columns].astype(jnp.float32), axis=0)
    own = own.astype(jnp.bfloat16).astype(jnp.float32)
    squares = jnp.sum(own * own, axis=1, keepdims=True)
    high = squares.astype(jnp.bfloat16).astype(jnp.float32)
    lane = lax.broadcasted_iota(jnp.int32, (rows, stream_own.shape[1] - columns), 1)
    split = jnp.where(lane == 0, high, jnp.where(lane == 1, squares - high, 0.0))
    stream_own[...] = jnp.concatenate([own, split], axis=1).astype(jnp.bfloat16)

    arrive = exchange("tp", 4, lambda to: stream_own, stream_rows, tp)
    stream_rows[tp] = stream_own[...]
    for load in loads[3:5]:
        load.wait()
    gain_swap()
    gate_swap()
    up_swap()
    arrive()
    finish.append(send(stream_rows.at[2 * z + 1 - core], base, other_core, 6).wait_send)
    base_arrive = pltpu.make_async_copy(base, base, recv_sem.at[6]).wait
    scaled, tail = [], 0.0
    for side in range(2):
        part = jnp.stack([stream_rows[2 * k + side] for k in range(chips)])
        part = part.astype(jnp.float32)
        tail += part[:, :, columns // 128 * 128 :]
        part = part[:, :, :columns].reshape(chips * rows, columns)
        scaled.append((part * gains[side, :1, :columns].astype(jnp.float32)).astype(jnp.bfloat16))

    first = hidden_block.shape[1]
    parts = [
        (slice(0, first), (first_send, first_recv)),
        (slice(first, units), (second_send, second_recv)),
    ]
    arrivals = []
    for part, (some, (block, recv)) in enumerate(parts):
        at = 0
        for held_weight in (gate_held, up_held):
            product = sum(
                jnp.dot(
                    scaled[side], held_weight[side, :, some], preferred_element_type=jnp.float32
                )
                for side in range(2)
            )
            product = product.astype(jnp.bfloat16).reshape(chips, rows, -1)
            block[:, :, at : at + product.shape[2]] = product
            at += product.shape[2]
        if part == 0:
            block[:, :, at:] = tail.astype(jnp.bfloat16)
        arrivals.append(exchange("dp", 7 + part, lambda to: block.at[to], recv, chip))
        recv[chip] = block[chip]
    gathers = []
    for part, (arrive, (some, refs)) in enumerate(zip(arrivals, parts)):
        width = some.stop - some.start
        arrive()
        sums = jnp.sum(refs[1][...].astype(jnp.float32), axis=0)
        if part == 0:
            at = 2 * width + columns % 128
            squares = sums[:, at : at + 1] + sums[:, at + 1 : at + 2]
            inv_rms = 1.0 / jnp.sqrt(squares / model + 1e-06)
        gate = sums[:, :width] * inv_rms
        up = sums[:, width : 2 * width] * inv_rms
        hidden = gate / (1.0 + jnp.exp(-gate)) * up
        block, target = ((hidden_block, hidden_rows), (rest_block, rest_rows))[part]
        block[...] = hidden.astype(jnp.bfloat16)
        gathers.append(gather(1 + part, block, target))

    loads[5].wait()
    down_swap()
    down = [0.0, 0.0]
    sides = (1 - core, core)
    for arrive, target, (some, _) in zip(gathers, (hidden_rows, rest_rows), parts):
        arrive()
        hidden = target[...].reshape(chips * rows, -1)
        for at, side in enumerate(sides):
            down[at] += lax.dot_general(
                hidden, down_held[side, :, some], NT, preferred_element_type=jnp.float32
            )

    def down_blocks(at):
        product = down[at].astype(jnp.bfloat16).reshape(chips, rows, columns)
        down_send[sides[at], :, :, :columns] = product

    def scatter(blocks, half):
        for dz in sorted(range(8), key=lambda d: -min(d, 8 - d)):
            k = lax.rem(z + dz, 8)
            to = 2 * k + half

            def give(k=k, to=to):
                send(blocks.at[k], down_recv.at[tp], {"tp": to}, 5)

            if dz:
                give()
            else:
                pl.when(to != tp)(give)

                @pl.when(to == tp)
                def _():
                    down_recv[tp] = blocks[z]

    down_blocks(0)
    finish.append(send(down_send.at[1 - core], down_other, other_core, 15).wait_send)
    down_blocks(1)
    scatter(down_send.at[core], core)
    pltpu.make_async_copy(down_other, down_other, recv_sem.at[15]).wait()
    scatter(down_other, 1 - core)
    blocks = down_recv.at[: groups - 1]
    finish.append(pltpu.make_async_copy(blocks, blocks, send_sem.at[5]).wait)
    pltpu.make_async_copy(blocks, blocks, recv_sem.at[5]).wait()
    base_arrive()
    stream = jnp.where(core == x_lo, stream_rows[2 * z + core], base[...])[:, :columns]
    result = jnp.sum(down_recv[:, :, :columns].astype(jnp.float32), axis=0)
    mixed[...] = (stream.astype(jnp.float32) + result).astype(jnp.bfloat16)
    for sent in finish:
        sent()


def layer(
    lengths,
    cache,
    w_value,
    queries,
    sums,
    stats,
    w_out,
    residual,
    gain,
    w_gate,
    w_up,
    w_down,
    groups,
    model,
):
    rows, heads, depth = queries.shape
    columns, units = w_down.shape
    wide = -(-columns // 128) * 128
    rest = units // 256 * 128
    first = units - rest
    vmem = pl.BlockSpec(memory_space=pltpu.VMEM)
    anywhere = pl.BlockSpec(memory_space=pl.ANY)
    blocks = lambda width: pltpu.VMEM((groups, rows, width), jnp.bfloat16)
    half = lambda width: pltpu.VMEM((groups // 2, rows, width), jnp.bfloat16)
    sides = lambda width: pltpu.VMEM((groups // 2, 2, rows, width), jnp.bfloat16)
    both = lambda array: pltpu.VMEM((2, *array.shape), jnp.bfloat16)
    return pl.pallas_call(
        functools.partial(layer_kernel, model),
        out_shape=jax.ShapeDtypeStruct((rows, columns), jnp.bfloat16),
        in_specs=[anywhere] * 12,
        out_specs=vmem,
        scratch_shapes=[
            pltpu.SMEM(lengths.shape, jnp.int32),
            pltpu.VMEM((rows, depth, FIRST), jnp.bfloat16),
            pltpu.VMEM(w_value.shape, jnp.bfloat16),
            pltpu.VMEM(queries.shape, jnp.bfloat16),
            pltpu.VMEM(sums.shape, jnp.float32),
            pltpu.VMEM(stats.shape, jnp.float32),
            pltpu.VMEM((heads, rows, KVR), jnp.float32),
            pltpu.VMEM((rows, heads * VD), jnp.bfloat16),
            both(w_out),
            both(w_gate),
            both(w_up),
            both(w_down),
            both(residual),
            pltpu.VMEM(gain.shape, jnp.bfloat16),
            pltpu.VMEM((2, *residual.shape[::-1]), jnp.float32),
            half(heads * VD),
            sides(wide),
            blocks(wide),
            pltpu.VMEM((2, rows, wide), jnp.bfloat16),
            pltpu.VMEM((rows, wide), jnp.bfloat16),
            blocks(wide),
            pltpu.VMEM((rows, wide), jnp.bfloat16),
            half(2 * first + 128),
            half(2 * first + 128),
            half(2 * rest),
            half(2 * rest),
            pltpu.VMEM((rows, first), jnp.bfloat16),
            half(first),
            pltpu.VMEM((rows, rest), jnp.bfloat16),
            half(rest),
            pltpu.VMEM((2, groups // 2, rows, wide), jnp.bfloat16),
            half(wide),
            blocks(wide),
            pltpu.SemaphoreType.DMA((5,)),
            pltpu.SemaphoreType.DMA((rows,)),
            pltpu.SemaphoreType.DMA((6,)),
            pltpu.SemaphoreType.DMA((16,)),
            pltpu.SemaphoreType.DMA((16,)),
        ],
        compiler_params=pltpu.CompilerParams(
            collective_id=0, has_side_effects=True, vmem_limit_bytes=VMEM_BYTES
        ),
        name="layer",
    )(
        lengths,
        cache,
        w_value,
        queries,
        sums,
        stats,
        w_out,
        residual,
        gain,
        w_gate,
        w_up,
        w_down,
    )


def solution(mesh):
    groups = mesh.shape["dp"]

    def on_device(
        query,
        latent_cache,
        lengths,
        w_uk,
        value_up_weight,
        w_out,
        residual,
        mlp_norm_scale,
        w_gate,
        w_up,
        w_down,
    ):
        cache = jnp.swapaxes(latent_cache, 1, 2)
        queries, sums, stats = attend_later(query, cache, lengths, w_uk)
        return layer(
            lengths,
            cache,
            value_up_weight,
            queries,
            sums,
            stats,
            w_out.T,
            residual.T,
            mlp_norm_scale,
            w_gate,
            w_up,
            w_down.T,
            groups,
            groups * mlp_norm_scale.shape[0],
        )

    return jax.shard_map(
        on_device,
        mesh=mesh,
        in_specs=(
            P("dp", "tp"),
            P("dp", None, None),
            P("dp"),
            P("tp", None, None),
            P("tp", None, None),
            P("tp", "dp"),
            P(None, "dp"),
            P("dp"),
            P("dp", "tp"),
            P("dp", "tp"),
            P("tp", "dp"),
        ),
        out_specs=P("tp", "dp"),
        check_vma=False,
    )
```

```python
import functools

import jax
import jax.numpy as jnp
from jax import lax
from jax.experimental import pallas as pl
from jax.experimental.pallas import tpu as pltpu
from jax.sharding import PartitionSpec as P

CHIP_PEERS = sorted(
    [(a, b) for a in range(2) for b in range(4) if a + b],
    key=lambda d: -(2 * d[0] + min(d[1], 4 - d[1])),
)
TP_PEERS = sorted(
    [(a, b) for a in range(8) for b in range(2) if a + b],
    key=lambda d: -(min(d[0], 8 - d[0]) + d[1]),
)
MESH = pl.DeviceIdType.MESH
NOPE = 128
ROPE = 64
KVR = 512
VD = 128
FIRST = 512
TOGETHER = 4
VMEM_BYTES = 60 * 2**20
NT = (((1,), (1,)), ((), ()))


def project(query, w_uk, queries):
    width = NOPE + ROPE
    for h in range(w_uk.shape[0]):
        nope = query[:, h * width : h * width + NOPE]
        queries[:, h, :KVR] = jnp.dot(nope, w_uk[h], preferred_element_type=jnp.float32)
        queries[:, h, KVR:] = query[:, h * width + NOPE : (h + 1) * width].astype(jnp.float32)


def live_scores(query, keys, first, length):
    got = jnp.dot(query, keys, preferred_element_type=jnp.float32)
    at = first + lax.broadcasted_iota(jnp.int32, got.shape, 1)
    return jnp.where(at < length, got * (1.0 / jnp.sqrt(jnp.float32(NOPE + ROPE))), -jnp.inf)


def weighted(probs, keys):
    return lax.dot_general(
        probs.astype(jnp.bfloat16), keys, NT, preferred_element_type=jnp.float32
    )


def later_kernel(
    lengths_in,
    query_in,
    cache,
    w_uk,
    queries,
    sums,
    stats,
    lengths,
    query,
    held,
    uk_held,
    wide_queries,
    cache_sem,
    load_sem,
):
    requests = queries.shape[0]
    most = cache.shape[2] // FIRST - 1
    loads = [
        pltpu.make_async_copy(src, dst, load_sem.at[at])
        for at, (src, dst) in enumerate(
            [(lengths_in, lengths), (w_uk, uk_held), (query_in, query)]
        )
    ]
    for load in loads:
        load.start()
    sums[...] = jnp.zeros_like(sums)
    stats[0] = jnp.full(stats.shape[1:], -1e30, jnp.float32)
    stats[1] = jnp.zeros(stats.shape[1:], jnp.float32)
    loads[0].wait()

    def each(step):
        @pl.loop(0, requests)
        def _(b):
            chunks = lax.div(lengths[b] - 1, FIRST)

            @pl.when(chunks > 0)
            def _():
                for k in range(1, most + 1):
                    pl.when(chunks == k)(lambda k=k: step(b, k * FIRST))

    def copy(b, width):
        return pltpu.make_async_copy(
            cache.at[b, :, FIRST : FIRST + width], held.at[b, :, :width], cache_sem.at[b]
        )

    each(lambda b, width: copy(b, width).start())
    loads[1].wait()
    loads[2].wait()
    project(query, uk_held, wide_queries)
    queries[...] = wide_queries[...].astype(jnp.bfloat16)
    longest = lengths[0]
    for b in range(1, requests):
        longest = jnp.maximum(longest, lengths[b])

    @pl.when(longest > FIRST)
    def _():
        def step(b, width):
            copy(b, width).wait()
            scores = live_scores(queries[b], held[b, :, :width], FIRST, lengths[b])
            top = jnp.max(scores, axis=1, keepdims=True)
            probs = jnp.exp(scores - top)
            total = jnp.sum(probs, axis=1, keepdims=True)
            sums[b] = weighted(probs, held[b, :KVR, :width])
            stats[0, b] = jnp.broadcast_to(top, stats.shape[2:])
            stats[1, b] = jnp.broadcast_to(total, stats.shape[2:])

        each(step)


def attend_later(query, cache, lengths, w_uk):
    requests, depth, slots = cache.shape
    heads = w_uk.shape[0]
    vmem = pl.BlockSpec(memory_space=pltpu.VMEM)
    anywhere = pl.BlockSpec(memory_space=pl.ANY)
    return pl.pallas_call(
        later_kernel,
        out_shape=[
            jax.ShapeDtypeStruct((requests, heads, depth), jnp.bfloat16),
            jax.ShapeDtypeStruct((requests, heads, KVR), jnp.float32),
            jax.ShapeDtypeStruct((2, requests, heads, 128), jnp.float32),
        ],
        in_specs=[anywhere] * 4,
        out_specs=[vmem] * 3,
        scratch_shapes=[
            pltpu.SMEM(lengths.shape, jnp.int32),
            pltpu.VMEM(query.shape, jnp.bfloat16),
            pltpu.VMEM((requests, depth, slots - FIRST), jnp.bfloat16),
            pltpu.VMEM(w_uk.shape, jnp.bfloat16),
            pltpu.VMEM((requests, heads, depth), jnp.float32),
            pltpu.SemaphoreType.DMA((requests,)),
            pltpu.SemaphoreType.DMA((3,)),
        ],
        compiler_params=pltpu.CompilerParams(vmem_limit_bytes=VMEM_BYTES),
        name="attend_later",
    )(lengths, query, cache, w_uk)


def layer_kernel(
    model,
    lengths_in,
    cache,
    w_value,
    queries_in,
    sums_in,
    stats_in,
    w_out,
    residual,
    gain_in,
    w_gate,
    w_up,
    w_down,
    mixed,
    lengths,
    held,
    value_held,
    queries,
    sums,
    stats,
    context,
    values,
    out_held,
    gate_held,
    up_held,
    down_held,
    out_turned,
    down_turned,
    residual_held,
    gain,
    residual_rows,
    all_values,
    out_send,
    out_recv,
    gains,
    stream_own,
    stream_rows,
    base,
    first_send,
    first_recv,
    second_send,
    second_recv,
    hidden_block,
    hidden_rows,
    rest_block,
    rest_rows,
    down_send,
    down_recv,
    attend_sem,
    cache_sem,
    weight_sem,
    send_sem,
    recv_sem,
):
    dp, tp = lax.axis_index("dp"), lax.axis_index("tp")
    groups = out_recv.shape[0]
    rows = values.shape[0]
    columns = mixed.shape[1]
    units = gate_held.shape[2]
    chips = groups // 2

    chip = dp // 2
    core, y, x_hi = lax.rem(dp, 2), lax.rem(dp // 2, 4), dp // 8
    x_lo, z = lax.rem(tp, 2), tp // 2
    requests = cache.shape[0]
    attend_loads = [
        pltpu.make_async_copy(src, dst, attend_sem.at[at])
        for at, (src, dst) in enumerate(
            [
                (queries_in, queries),
                (lengths_in, lengths),
                (stats_in, stats),
                (sums_in, sums),
                (w_value, value_held),
            ]
        )
    ]
    cache_loads = [
        pltpu.make_async_copy(cache.at[b, :, :FIRST], held.at[b], cache_sem.at[b])
        for b in range(requests)
    ]
    loads = [
        pltpu.make_async_copy(src, dst, weight_sem.at[at])
        for at, (src, dst) in enumerate(
            [
                (w_out, out_held.at[core]),
                (residual, residual_held.at[core]),
                (gain_in, gain),
                (w_gate, gate_held.at[core]),
                (w_up, up_held.at[core]),
                (w_down, down_held.at[core]),
            ]
        )
    ]
    for load in attend_loads[:4] + cache_loads + attend_loads[4:] + loads:
        load.start()

    def along(axis, d):
        if axis == "dp":
            return {"dp": lax.rem(x_hi + d[0], 2) * 8 + lax.rem(y + d[1], 4) * 2 + core}
        return {"tp": lax.rem(z + d[0], 8) * 2 + lax.rem(x_lo + d[1], 2)}

    other_dp = chip * 2 + 1 - core
    other_core = {"dp": other_dp, "tp": tp}
    barrier = pltpu.get_barrier_semaphore()
    partners = [along("dp", d) for d in CHIP_PEERS] + [along("tp", d) for d in TP_PEERS]
    partners += [{"dp": other_dp, **along("tp", d)} for d in TP_PEERS] + [other_core]
    for partner in partners:
        pl.semaphore_signal(barrier, inc=1, device_id=partner, device_id_type=MESH)

    for load in attend_loads[:4]:
        load.wait()

    def finish_request(b, scores):
        later = stats[0, b, :, :1]
        top = jnp.maximum(jnp.max(scores, axis=1, keepdims=True), later)
        share = jnp.exp(later - top)
        probs = jnp.exp(scores - top)
        total = jnp.sum(probs, axis=1, keepdims=True) + stats[1, b, :, :1] * share
        context[:, b, :] = (weighted(probs, held[b, :KVR, :]) + sums[b] * share) * (1.0 / total)

    before = []
    for first in range(0, requests, TOGETHER):
        some = range(first, first + TOGETHER)
        for b in some:
            cache_loads[b].wait()
        now = [(b, live_scores(queries[b], held[b], 0, lengths[b])) for b in some]
        for b, scores in before:
            finish_request(b, scores)
        before = now
    for b, scores in before:
        finish_request(b, scores)
    attend_loads[4].wait()
    for h in range(value_held.shape[0]):
        values[:, h * VD : (h + 1) * VD] = jnp.dot(
            context[h].astype(jnp.bfloat16), value_held[h], preferred_element_type=jnp.float32
        ).astype(jnp.bfloat16)

    pl.semaphore_wait(barrier, len(partners))
    finish = []

    def send(block, place, device, phase):
        copy = pltpu.make_async_remote_copy(
            src_ref=block,
            dst_ref=place,
            send_sem=send_sem.at[phase],
            recv_sem=recv_sem.at[phase],
            device_id=device,
            device_id_type=MESH,
        )
        copy.start()
        return copy

    def exchange(axis, phase, source, target, place):
        peers = CHIP_PEERS if axis == "dp" else TP_PEERS
        for d in peers:
            to = along(axis, d)
            at = to["dp"] // 2 if axis == "dp" else to["tp"]
            send(source(at), target.at[place], to, phase)
        blocks = target.at[: len(peers)]
        finish.append(pltpu.make_async_copy(blocks, blocks, send_sem.at[phase]).wait)
        return pltpu.make_async_copy(blocks, blocks, recv_sem.at[phase]).wait

    def gather(phase, block, target):
        arrive = exchange("dp", phase, lambda to: block, target, chip)
        target[chip] = block[...]
        return arrive

    def swap(phase, source, held):
        finish.append(send(source, held.at[core], other_core, phase).wait_send)
        theirs = held.at[1 - core]
        return pltpu.make_async_copy(theirs, theirs, recv_sem.at[phase]).wait

    arrive = gather(0, values, all_values)
    loads[2].wait()
    own_gain = gain[...].astype(jnp.float32)[None, :]
    gains[core, :, :columns] = jnp.broadcast_to(own_gain, (rows, columns)).astype(jnp.bfloat16)
    out_swap = swap(9, w_out, out_held)
    residual_swap = swap(10, residual, residual_held)
    gain_swap = swap(11, gains.at[core], gains)
    gate_swap = swap(12, w_gate, gate_held)
    up_swap = swap(13, w_up, up_held)
    down_swap = swap(14, w_down, down_held)
    loads[1].wait()
    residual_swap()
    for side in range(2):
        residual_rows[side] = residual_held[side].astype(jnp.float32).T
    loads[0].wait()
    out_turned[core] = out_held[core].T
    out_swap()
    out_turned[1 - core] = out_held[1 - core].T
    arrive()
    every = all_values[...].reshape(chips * rows, -1)
    for side in range(2):
        attended = jnp.dot(every, out_turned[side], preferred_element_type=jnp.float32)
        attended = attended.astype(jnp.bfloat16).reshape(chips, rows, columns)
        out_send[:, side, :, :columns] = attended

    arrive = exchange("tp", 3, lambda to: out_send.at[to // 2, lax.rem(to, 2)], out_recv, tp)
    out_recv[tp] = out_send[z, x_lo]
    arrive()
    own_rows = pl.ds(pl.multiple_of((2 * z + core) * rows, rows), rows)
    own = residual_rows[x_lo, own_rows, :]
    own = own + jnp.sum(out_recv[:, :, :columns].astype(jnp.float32), axis=0)
    own = own.astype(jnp.bfloat16).astype(jnp.float32)
    squares = jnp.sum(own * own, axis=1, keepdims=True)
    high = squares.astype(jnp.bfloat16).astype(jnp.float32)
    lane = lax.broadcasted_iota(jnp.int32, (rows, stream_own.shape[1] - columns), 1)
    split = jnp.where(lane == 0, high, jnp.where(lane == 1, squares - high, 0.0))
    stream_own[...] = jnp.concatenate([own, split], axis=1).astype(jnp.bfloat16)

    arrive = exchange("tp", 4, lambda to: stream_own, stream_rows, tp)
    stream_rows[tp] = stream_own[...]
    for load in loads[3:5]:
        load.wait()
    gain_swap()
    gate_swap()
    up_swap()
    arrive()
    finish.append(send(stream_rows.at[2 * z + 1 - core], base, other_core, 6).wait_send)
    base_arrive = pltpu.make_async_copy(base, base, recv_sem.at[6]).wait
    scaled, tail = [], 0.0
    for side in range(2):
        part = jnp.stack([stream_rows[2 * k + side] for k in range(chips)])
        part = part.astype(jnp.float32)
        tail += part[:, :, columns // 128 * 128 :]
        part = part[:, :, :columns].reshape(chips * rows, columns)
        scaled.append((part * gains[side, :1, :columns].astype(jnp.float32)).astype(jnp.bfloat16))

    first = hidden_block.shape[1]
    parts = [
        (slice(0, first), (first_send, first_recv)),
        (slice(first, units), (second_send, second_recv)),
    ]
    arrivals = []
    for part, (some, (block, recv)) in enumerate(parts):
        at = 0
        for held_weight in (gate_held, up_held):
            product = sum(
                jnp.dot(
                    scaled[side], held_weight[side, :, some], preferred_element_type=jnp.float32
                )
                for side in range(2)
            )
            product = product.astype(jnp.bfloat16).reshape(chips, rows, -1)
            block[:, :, at : at + product.shape[2]] = product
            at += product.shape[2]
        if part == 0:
            block[:, :, at:] = tail.astype(jnp.bfloat16)
        arrivals.append(exchange("dp", 7 + part, lambda to: block.at[to], recv, chip))
        recv[chip] = block[chip]
    loads[5].wait()
    down_swap()
    for side in range(2):
        down_turned[side] = down_held[side].T
    gathers = []
    for part, (arrive, (some, refs)) in enumerate(zip(arrivals, parts)):
        width = some.stop - some.start
        arrive()
        sums = jnp.sum(refs[1][...].astype(jnp.float32), axis=0)
        if part == 0:
            at = 2 * width + columns % 128
            squares = sums[:, at : at + 1] + sums[:, at + 1 : at + 2]
            inv_rms = 1.0 / jnp.sqrt(squares / model + 1e-06)
        gate = sums[:, :width] * inv_rms
        up = sums[:, width : 2 * width] * inv_rms
        hidden = gate / (1.0 + jnp.exp(-gate)) * up
        block, target = ((hidden_block, hidden_rows), (rest_block, rest_rows))[part]
        block[...] = hidden.astype(jnp.bfloat16)
        gathers.append(gather(1 + part, block, target))

    down = [0.0, 0.0]
    for arrive, target, (some, _) in zip(gathers, (hidden_rows, rest_rows), parts):
        arrive()
        hidden = target[...].reshape(chips * rows, -1)
        for side in range(2):
            down[side] += jnp.dot(
                hidden, down_turned[side, some, :], preferred_element_type=jnp.float32
            )
    for side in range(2):
        product = down[side].astype(jnp.bfloat16).reshape(chips, rows, columns)
        down_send[:, side, :, :columns] = product

    kept = core == x_lo
    for dz in sorted(range(8), key=lambda d: -min(d, 8 - d)):
        k = lax.rem(z + dz, 8)
        for side in (1 - core, core):
            device = {"dp": chip * 2 + side, "tp": 2 * k + core}

            def give(phase, k=k, side=side, device=device):
                send(down_send.at[k, side], down_recv.at[tp], device, phase)

            if dz == 0 and side is core:
                pl.when(jnp.logical_not(kept))(lambda give=give: give(15))
            else:
                give(5)

    @pl.when(kept)
    def _():
        down_recv[tp] = down_send[z, core]

    def wait_down(sem, blocks):
        blocks = down_recv.at[:blocks]
        pltpu.make_async_copy(blocks, blocks, sem).wait()

    @pl.when(kept)
    def _():
        wait_down(recv_sem.at[5], groups - 2)
        wait_down(recv_sem.at[15], 1)

    @pl.when(jnp.logical_not(kept))
    def _():
        wait_down(recv_sem.at[5], groups)

    base_arrive()
    stream = jnp.where(kept, stream_rows[2 * z + core], base[...])[:, :columns]
    result = jnp.sum(down_recv[:, :, :columns].astype(jnp.float32), axis=0)
    mixed[...] = (stream.astype(jnp.float32) + result).astype(jnp.bfloat16)
    wait_down(send_sem.at[5], groups - 1)
    pl.when(jnp.logical_not(kept))(lambda: wait_down(send_sem.at[15], 1))
    for sent in finish:
        sent()


def layer(
    lengths,
    cache,
    w_value,
    queries,
    sums,
    stats,
    w_out,
    residual,
    gain,
    w_gate,
    w_up,
    w_down,
    groups,
    model,
):
    rows, heads, depth = queries.shape
    columns, units = w_down.shape
    wide = -(-columns // 128) * 128
    rest = units // 256 * 128
    first = units - rest
    vmem = pl.BlockSpec(memory_space=pltpu.VMEM)
    anywhere = pl.BlockSpec(memory_space=pl.ANY)
    blocks = lambda width: pltpu.VMEM((groups, rows, width), jnp.bfloat16)
    half = lambda width: pltpu.VMEM((groups // 2, rows, width), jnp.bfloat16)
    sides = lambda width: pltpu.VMEM((groups // 2, 2, rows, width), jnp.bfloat16)
    both = lambda array: pltpu.VMEM((2, *array.shape), jnp.bfloat16)
    return pl.pallas_call(
        functools.partial(layer_kernel, model),
        out_shape=jax.ShapeDtypeStruct((rows, columns), jnp.bfloat16),
        in_specs=[anywhere] * 12,
        out_specs=vmem,
        scratch_shapes=[
            pltpu.SMEM(lengths.shape, jnp.int32),
            pltpu.VMEM((rows, depth, FIRST), jnp.bfloat16),
            pltpu.VMEM(w_value.shape, jnp.bfloat16),
            pltpu.VMEM(queries.shape, jnp.bfloat16),
            pltpu.VMEM(sums.shape, jnp.float32),
            pltpu.VMEM(stats.shape, jnp.float32),
            pltpu.VMEM((heads, rows, KVR), jnp.float32),
            pltpu.VMEM((rows, heads * VD), jnp.bfloat16),
            both(w_out),
            both(w_gate),
            both(w_up),
            both(w_down),
            pltpu.VMEM((2, *w_out.shape[::-1]), jnp.bfloat16),
            pltpu.VMEM((2, *w_down.shape[::-1]), jnp.bfloat16),
            both(residual),
            pltpu.VMEM(gain.shape, jnp.bfloat16),
            pltpu.VMEM((2, *residual.shape[::-1]), jnp.float32),
            half(heads * VD),
            sides(wide),
            blocks(wide),
            pltpu.VMEM((2, rows, wide), jnp.bfloat16),
            pltpu.VMEM((rows, wide), jnp.bfloat16),
            blocks(wide),
            pltpu.VMEM((rows, wide), jnp.bfloat16),
            half(2 * first + 128),
            half(2 * first + 128),
            half(2 * rest),
            half(2 * rest),
            pltpu.VMEM((rows, first), jnp.bfloat16),
            half(first),
            pltpu.VMEM((rows, rest), jnp.bfloat16),
            half(rest),
            sides(wide),
            blocks(wide),
            pltpu.SemaphoreType.DMA((5,)),
            pltpu.SemaphoreType.DMA((rows,)),
            pltpu.SemaphoreType.DMA((6,)),
            pltpu.SemaphoreType.DMA((16,)),
            pltpu.SemaphoreType.DMA((16,)),
        ],
        compiler_params=pltpu.CompilerParams(
            collective_id=0, has_side_effects=True, vmem_limit_bytes=VMEM_BYTES
        ),
        name="layer",
    )(
        lengths,
        cache,
        w_value,
        queries,
        sums,
        stats,
        w_out,
        residual,
        gain,
        w_gate,
        w_up,
        w_down,
    )


def solution(mesh):
    groups = mesh.shape["dp"]

    def on_device(
        query,
        latent_cache,
        lengths,
        w_uk,
        value_up_weight,
        w_out,
        residual,
        mlp_norm_scale,
        w_gate,
        w_up,
        w_down,
    ):
        cache = jnp.swapaxes(latent_cache, 1, 2)
        queries, sums, stats = attend_later(query, cache, lengths, w_uk)
        return layer(
            lengths,
            cache,
            value_up_weight,
            queries,
            sums,
            stats,
            w_out.T,
            residual.T,
            mlp_norm_scale,
            w_gate,
            w_up,
            w_down.T,
            groups,
            groups * mlp_norm_scale.shape[0],
        )

    return jax.shard_map(
        on_device,
        mesh=mesh,
        in_specs=(
            P("dp", "tp"),
            P("dp", None, None),
            P("dp"),
            P("tp", None, None),
            P("tp", None, None),
            P("tp", "dp"),
            P(None, "dp"),
            P("dp"),
            P("dp", "tp"),
            P("dp", "tp"),
            P("tp", "dp"),
        ),
        out_specs=P("tp", "dp"),
        check_vma=False,
    )
```

```python
import functools

import jax
import jax.numpy as jnp
from jax import lax
from jax.experimental import pallas as pl
from jax.experimental.pallas import tpu as pltpu
from jax.sharding import PartitionSpec as P

CHIP_PEERS = sorted(
    [(a, b) for a in range(2) for b in range(4) if a + b],
    key=lambda d: -(2 * d[0] + min(d[1], 4 - d[1])),
)
TP_PEERS = sorted(
    [(a, b) for a in range(8) for b in range(2) if a + b],
    key=lambda d: -(min(d[0], 8 - d[0]) + d[1]),
)
MESH = pl.DeviceIdType.MESH
NOPE = 128
ROPE = 64
KVR = 512
VD = 128
FIRST = 512
TOGETHER = 4
VMEM_BYTES = 60 * 2**20
NT = (((1,), (1,)), ((), ()))


def project(query, w_uk, queries):
    width = NOPE + ROPE
    for h in range(w_uk.shape[0]):
        nope = query[:, h * width : h * width + NOPE]
        queries[:, h, :KVR] = jnp.dot(nope, w_uk[h], preferred_element_type=jnp.float32)
        queries[:, h, KVR:] = query[:, h * width + NOPE : (h + 1) * width].astype(jnp.float32)


def live_scores(query, keys, first, length):
    got = jnp.dot(query, keys, preferred_element_type=jnp.float32)
    at = first + lax.broadcasted_iota(jnp.int32, got.shape, 1)
    return jnp.where(at < length, got * (1.0 / jnp.sqrt(jnp.float32(NOPE + ROPE))), -jnp.inf)


def weighted(probs, keys):
    return lax.dot_general(
        probs.astype(jnp.bfloat16), keys, NT, preferred_element_type=jnp.float32
    )


def later_kernel(
    lengths_in,
    query_in,
    cache,
    w_uk,
    queries,
    sums,
    stats,
    lengths,
    query,
    held,
    uk_held,
    wide_queries,
    cache_sem,
    load_sem,
):
    requests = queries.shape[0]
    most = cache.shape[2] // FIRST - 1
    loads = [
        pltpu.make_async_copy(src, dst, load_sem.at[at])
        for at, (src, dst) in enumerate(
            [(lengths_in, lengths), (w_uk, uk_held), (query_in, query)]
        )
    ]
    for load in loads:
        load.start()
    sums[...] = jnp.zeros_like(sums)
    stats[0] = jnp.full(stats.shape[1:], -1e30, jnp.float32)
    stats[1] = jnp.zeros(stats.shape[1:], jnp.float32)
    loads[0].wait()

    def each(step):
        @pl.loop(0, requests)
        def _(b):
            chunks = lax.div(lengths[b] - 1, FIRST)

            @pl.when(chunks > 0)
            def _():
                for k in range(1, most + 1):
                    pl.when(chunks == k)(lambda k=k: step(b, k * FIRST))

    def copy(b, width):
        return pltpu.make_async_copy(
            cache.at[b, :, FIRST : FIRST + width], held.at[b, :, :width], cache_sem.at[b]
        )

    each(lambda b, width: copy(b, width).start())
    loads[1].wait()
    loads[2].wait()
    project(query, uk_held, wide_queries)
    queries[...] = wide_queries[...].astype(jnp.bfloat16)
    longest = lengths[0]
    for b in range(1, requests):
        longest = jnp.maximum(longest, lengths[b])

    @pl.when(longest > FIRST)
    def _():
        def step(b, width):
            copy(b, width).wait()
            scores = live_scores(queries[b], held[b, :, :width], FIRST, lengths[b])
            top = jnp.max(scores, axis=1, keepdims=True)
            probs = jnp.exp(scores - top)
            total = jnp.sum(probs, axis=1, keepdims=True)
            sums[b] = weighted(probs, held[b, :KVR, :width])
            stats[0, b] = jnp.broadcast_to(top, stats.shape[2:])
            stats[1, b] = jnp.broadcast_to(total, stats.shape[2:])

        each(step)


def attend_later(query, cache, lengths, w_uk):
    requests, depth, slots = cache.shape
    heads = w_uk.shape[0]
    vmem = pl.BlockSpec(memory_space=pltpu.VMEM)
    anywhere = pl.BlockSpec(memory_space=pl.ANY)
    return pl.pallas_call(
        later_kernel,
        out_shape=[
            jax.ShapeDtypeStruct((requests, heads, depth), jnp.bfloat16),
            jax.ShapeDtypeStruct((requests, heads, KVR), jnp.float32),
            jax.ShapeDtypeStruct((2, requests, heads, 128), jnp.float32),
        ],
        in_specs=[anywhere] * 4,
        out_specs=[vmem] * 3,
        scratch_shapes=[
            pltpu.SMEM(lengths.shape, jnp.int32),
            pltpu.VMEM(query.shape, jnp.bfloat16),
            pltpu.VMEM((requests, depth, slots - FIRST), jnp.bfloat16),
            pltpu.VMEM(w_uk.shape, jnp.bfloat16),
            pltpu.VMEM((requests, heads, depth), jnp.float32),
            pltpu.SemaphoreType.DMA((requests,)),
            pltpu.SemaphoreType.DMA((3,)),
        ],
        compiler_params=pltpu.CompilerParams(vmem_limit_bytes=VMEM_BYTES),
        name="attend_later",
    )(lengths, query, cache, w_uk)


def layer_kernel(
    model,
    lengths_in,
    cache,
    w_value,
    queries_in,
    sums_in,
    stats_in,
    w_out,
    residual,
    gain_in,
    w_gate,
    w_up,
    w_down,
    mixed,
    lengths,
    held,
    value_held,
    queries,
    sums,
    stats,
    context,
    values,
    out_held,
    gate_held,
    up_held,
    down_held,
    out_turned,
    down_turned,
    residual_held,
    gain,
    residual_rows,
    all_values,
    out_send,
    out_recv,
    gains,
    stream_own,
    stream_rows,
    base,
    first_send,
    first_recv,
    second_send,
    second_recv,
    hidden_block,
    hidden_rows,
    rest_block,
    rest_rows,
    down_send,
    down_recv,
    attend_sem,
    cache_sem,
    weight_sem,
    send_sem,
    recv_sem,
):
    dp, tp = lax.axis_index("dp"), lax.axis_index("tp")
    groups = out_recv.shape[0]
    rows = values.shape[0]
    columns = mixed.shape[1]
    units = gate_held.shape[2]
    chips = groups // 2

    chip = dp // 2
    core, y, x_hi = lax.rem(dp, 2), lax.rem(dp // 2, 4), dp // 8
    x_lo, z = lax.rem(tp, 2), tp // 2
    requests = cache.shape[0]
    attend_loads = [
        pltpu.make_async_copy(src, dst, attend_sem.at[at])
        for at, (src, dst) in enumerate(
            [
                (queries_in, queries),
                (lengths_in, lengths),
                (stats_in, stats),
                (sums_in, sums),
                (w_value, value_held),
            ]
        )
    ]
    cache_loads = [
        pltpu.make_async_copy(cache.at[b, :, :FIRST], held.at[b], cache_sem.at[b])
        for b in range(requests)
    ]
    loads = [
        pltpu.make_async_copy(src, dst, weight_sem.at[at])
        for at, (src, dst) in enumerate(
            [
                (w_out, out_held.at[core]),
                (residual, residual_held.at[core]),
                (gain_in, gain),
                (w_gate, gate_held.at[core]),
                (w_up, up_held.at[core]),
                (w_down, down_held.at[core]),
            ]
        )
    ]
    for load in attend_loads[:4] + cache_loads + attend_loads[4:] + loads:
        load.start()

    def along(axis, d):
        if axis == "dp":
            return {"dp": lax.rem(x_hi + d[0], 2) * 8 + lax.rem(y + d[1], 4) * 2 + core}
        return {"tp": lax.rem(z + d[0], 8) * 2 + lax.rem(x_lo + d[1], 2)}

    other_dp = chip * 2 + 1 - core
    other_core = {"dp": other_dp, "tp": tp}
    barrier = pltpu.get_barrier_semaphore()
    partners = [along("dp", d) for d in CHIP_PEERS] + [along("tp", d) for d in TP_PEERS]
    partners += [{"dp": other_dp, **along("tp", d)} for d in TP_PEERS] + [other_core]
    crossed = [{"dp": along("dp", d)["dp"] + 1 - 2 * core} for d in CHIP_PEERS]
    partners += crossed
    for partner in partners:
        pl.semaphore_signal(barrier, inc=1, device_id=partner, device_id_type=MESH)

    for load in attend_loads[:4]:
        load.wait()

    def finish_request(b, scores):
        later = stats[0, b, :, :1]
        top = jnp.maximum(jnp.max(scores, axis=1, keepdims=True), later)
        share = jnp.exp(later - top)
        probs = jnp.exp(scores - top)
        total = jnp.sum(probs, axis=1, keepdims=True) + stats[1, b, :, :1] * share
        context[:, b, :] = (weighted(probs, held[b, :KVR, :]) + sums[b] * share) * (1.0 / total)

    before = []
    for first in range(0, requests, TOGETHER):
        some = range(first, first + TOGETHER)
        for b in some:
            cache_loads[b].wait()
        now = [(b, live_scores(queries[b], held[b], 0, lengths[b])) for b in some]
        for b, scores in before:
            finish_request(b, scores)
        before = now
    for b, scores in before:
        finish_request(b, scores)
    attend_loads[4].wait()
    for h in range(value_held.shape[0]):
        values[:, h * VD : (h + 1) * VD] = jnp.dot(
            context[h].astype(jnp.bfloat16), value_held[h], preferred_element_type=jnp.float32
        ).astype(jnp.bfloat16)

    pl.semaphore_wait(barrier, len(partners))
    finish = []

    def send(block, place, device, phase):
        copy = pltpu.make_async_remote_copy(
            src_ref=block,
            dst_ref=place,
            send_sem=send_sem.at[phase],
            recv_sem=recv_sem.at[phase],
            device_id=device,
            device_id_type=MESH,
        )
        copy.start()
        return copy

    def exchange(axis, phase, source, target, place):
        peers = CHIP_PEERS if axis == "dp" else TP_PEERS
        for d in peers:
            to = along(axis, d)
            at = to["dp"] // 2 if axis == "dp" else to["tp"]
            send(source(at), target.at[place], to, phase)
        blocks = target.at[: len(peers)]
        finish.append(pltpu.make_async_copy(blocks, blocks, send_sem.at[phase]).wait)
        return pltpu.make_async_copy(blocks, blocks, recv_sem.at[phase]).wait

    def gather(phase, block, target):
        arrive = exchange("dp", phase, lambda to: block, target, chip)
        target[chip] = block[...]
        return arrive

    def swap(phase, source, held):
        finish.append(send(source, held.at[core], other_core, phase).wait_send)
        theirs = held.at[1 - core]
        return pltpu.make_async_copy(theirs, theirs, recv_sem.at[phase]).wait

    for device in crossed + [other_core]:
        send(values, all_values.at[chip], device, 0)
    finish.append(pltpu.make_async_copy(all_values, all_values, send_sem.at[0]).wait)
    arrive = pltpu.make_async_copy(all_values, all_values, recv_sem.at[0]).wait
    loads[2].wait()
    own_gain = gain[...].astype(jnp.float32)[None, :]
    gains[core, :, :columns] = jnp.broadcast_to(own_gain, (rows, columns)).astype(jnp.bfloat16)
    out_swap = swap(9, w_out, out_held)
    residual_swap = swap(10, residual, residual_held)
    gain_swap = swap(11, gains.at[core], gains)
    gate_swap = swap(12, w_gate, gate_held)
    up_swap = swap(13, w_up, up_held)
    down_swap = swap(14, w_down, down_held)
    loads[1].wait()
    residual_swap()
    for side in range(2):
        residual_rows[side] = residual_held[side].astype(jnp.float32).T
    loads[0].wait()
    out_turned[core] = out_held[core].T
    out_swap()
    out_turned[1 - core] = out_held[1 - core].T
    arrive()
    every = all_values[...].reshape(chips * rows, -1)
    for side in range(2):
        attended = jnp.dot(every, out_turned[side], preferred_element_type=jnp.float32)
        attended = attended.astype(jnp.bfloat16).reshape(chips, rows, columns)
        out_send[:, side, :, :columns] = attended

    arrive = exchange("tp", 3, lambda to: out_send.at[to // 2, lax.rem(to, 2)], out_recv, tp)
    out_recv[tp] = out_send[z, x_lo]
    arrive()
    own_rows = pl.ds(pl.multiple_of((2 * z + 1 - core) * rows, rows), rows)
    own = residual_rows[x_lo, own_rows, :]
    own = own + jnp.sum(out_recv[:, :, :columns].astype(jnp.float32), axis=0)
    own = own.astype(jnp.bfloat16).astype(jnp.float32)
    squares = jnp.sum(own * own, axis=1, keepdims=True)
    high = squares.astype(jnp.bfloat16).astype(jnp.float32)
    lane = lax.broadcasted_iota(jnp.int32, (rows, stream_own.shape[1] - columns), 1)
    split = jnp.where(lane == 0, high, jnp.where(lane == 1, squares - high, 0.0))
    stream_own[...] = jnp.concatenate([own, split], axis=1).astype(jnp.bfloat16)

    arrive = exchange("tp", 4, lambda to: stream_own, stream_rows, tp)
    stream_rows[tp] = stream_own[...]
    for load in loads[3:5]:
        load.wait()
    gain_swap()
    gate_swap()
    up_swap()
    arrive()
    finish.append(send(stream_rows.at[2 * z + 1 - core], base, other_core, 6).wait_send)
    base_arrive = pltpu.make_async_copy(base, base, recv_sem.at[6]).wait
    scaled, tail = [], 0.0
    for side in range(2):
        part = jnp.stack([stream_rows[2 * k + side] for k in range(chips)])
        part = part.astype(jnp.float32)
        tail += part[:, :, columns // 128 * 128 :]
        part = part[:, :, :columns].reshape(chips * rows, columns)
        scaled.append((part * gains[side, :1, :columns].astype(jnp.float32)).astype(jnp.bfloat16))

    first = hidden_block.shape[1]
    parts = [
        (slice(0, first), (first_send, first_recv)),
        (slice(first, units), (second_send, second_recv)),
    ]
    arrivals = []
    for part, (some, (block, recv)) in enumerate(parts):
        at = 0
        for held_weight in (gate_held, up_held):
            product = sum(
                jnp.dot(
                    scaled[side], held_weight[side, :, some], preferred_element_type=jnp.float32
                )
                for side in range(2)
            )
            product = product.astype(jnp.bfloat16).reshape(chips, rows, -1)
            block[:, :, at : at + product.shape[2]] = product
            at += product.shape[2]
        if part == 0:
            block[:, :, at:] = tail.astype(jnp.bfloat16)
        arrivals.append(exchange("dp", 7 + part, lambda to: block.at[to], recv, chip))
        recv[chip] = block[chip]
    loads[5].wait()
    down_swap()
    for side in range(2):
        down_turned[side] = down_held[side].T
    gathers = []
    for part, (arrive, (some, refs)) in enumerate(zip(arrivals, parts)):
        width = some.stop - some.start
        arrive()
        sums = jnp.sum(refs[1][...].astype(jnp.float32), axis=0)
        if part == 0:
            at = 2 * width + columns % 128
            squares = sums[:, at : at + 1] + sums[:, at + 1 : at + 2]
            inv_rms = 1.0 / jnp.sqrt(squares / model + 1e-06)
        gate = sums[:, :width] * inv_rms
        up = sums[:, width : 2 * width] * inv_rms
        hidden = gate / (1.0 + jnp.exp(-gate)) * up
        block, target = ((hidden_block, hidden_rows), (rest_block, rest_rows))[part]
        block[...] = hidden.astype(jnp.bfloat16)
        gathers.append(gather(1 + part, block, target))

    down = [0.0, 0.0]
    for arrive, target, (some, _) in zip(gathers, (hidden_rows, rest_rows), parts):
        arrive()
        hidden = target[...].reshape(chips * rows, -1)
        for side in range(2):
            down[side] += jnp.dot(
                hidden, down_turned[side, some, :], preferred_element_type=jnp.float32
            )
    for side in range(2):
        product = down[side].astype(jnp.bfloat16).reshape(chips, rows, columns)
        down_send[:, side, :, :columns] = product

    kept = core != x_lo
    for dz in sorted(range(8), key=lambda d: -min(d, 8 - d)):
        k = lax.rem(z + dz, 8)
        for side in (1 - core, core):
            device = {"dp": chip * 2 + side, "tp": 2 * k + 1 - core}

            def give(phase, k=k, side=side, device=device):
                send(down_send.at[k, side], down_recv.at[tp], device, phase)

            if dz == 0 and side is core:
                pl.when(jnp.logical_not(kept))(lambda give=give: give(15))
            else:
                give(5)

    @pl.when(kept)
    def _():
        down_recv[tp] = down_send[z, core]

    def wait_down(sem, blocks):
        blocks = down_recv.at[:blocks]
        pltpu.make_async_copy(blocks, blocks, sem).wait()

    @pl.when(kept)
    def _():
        wait_down(recv_sem.at[5], groups - 2)
        wait_down(recv_sem.at[15], 1)

    @pl.when(jnp.logical_not(kept))
    def _():
        wait_down(recv_sem.at[5], groups)

    base_arrive()
    stream = jnp.where(kept, stream_rows[2 * z + core], base[...])[:, :columns]
    result = jnp.sum(down_recv[:, :, :columns].astype(jnp.float32), axis=0)
    mixed[...] = (stream.astype(jnp.float32) + result).astype(jnp.bfloat16)
    wait_down(send_sem.at[5], groups - 1)
    pl.when(jnp.logical_not(kept))(lambda: wait_down(send_sem.at[15], 1))
    for sent in finish:
        sent()


def layer(
    lengths,
    cache,
    w_value,
    queries,
    sums,
    stats,
    w_out,
    residual,
    gain,
    w_gate,
    w_up,
    w_down,
    groups,
    model,
):
    rows, heads, depth = queries.shape
    columns, units = w_down.shape
    wide = -(-columns // 128) * 128
    rest = units // 256 * 128
    first = units - rest
    vmem = pl.BlockSpec(memory_space=pltpu.VMEM)
    anywhere = pl.BlockSpec(memory_space=pl.ANY)
    blocks = lambda width: pltpu.VMEM((groups, rows, width), jnp.bfloat16)
    half = lambda width: pltpu.VMEM((groups // 2, rows, width), jnp.bfloat16)
    sides = lambda width: pltpu.VMEM((groups // 2, 2, rows, width), jnp.bfloat16)
    both = lambda array: pltpu.VMEM((2, *array.shape), jnp.bfloat16)
    return pl.pallas_call(
        functools.partial(layer_kernel, model),
        out_shape=jax.ShapeDtypeStruct((rows, columns), jnp.bfloat16),
        in_specs=[anywhere] * 12,
        out_specs=vmem,
        scratch_shapes=[
            pltpu.SMEM(lengths.shape, jnp.int32),
            pltpu.VMEM((rows, depth, FIRST), jnp.bfloat16),
            pltpu.VMEM(w_value.shape, jnp.bfloat16),
            pltpu.VMEM(queries.shape, jnp.bfloat16),
            pltpu.VMEM(sums.shape, jnp.float32),
            pltpu.VMEM(stats.shape, jnp.float32),
            pltpu.VMEM((heads, rows, KVR), jnp.float32),
            pltpu.VMEM((rows, heads * VD), jnp.bfloat16),
            both(w_out),
            both(w_gate),
            both(w_up),
            both(w_down),
            pltpu.VMEM((2, *w_out.shape[::-1]), jnp.bfloat16),
            pltpu.VMEM((2, *w_down.shape[::-1]), jnp.bfloat16),
            both(residual),
            pltpu.VMEM(gain.shape, jnp.bfloat16),
            pltpu.VMEM((2, *residual.shape[::-1]), jnp.float32),
            half(heads * VD),
            sides(wide),
            blocks(wide),
            pltpu.VMEM((2, rows, wide), jnp.bfloat16),
            pltpu.VMEM((rows, wide), jnp.bfloat16),
            blocks(wide),
            pltpu.VMEM((rows, wide), jnp.bfloat16),
            half(2 * first + 128),
            half(2 * first + 128),
            half(2 * rest),
            half(2 * rest),
            pltpu.VMEM((rows, first), jnp.bfloat16),
            half(first),
            pltpu.VMEM((rows, rest), jnp.bfloat16),
            half(rest),
            sides(wide),
            blocks(wide),
            pltpu.SemaphoreType.DMA((5,)),
            pltpu.SemaphoreType.DMA((rows,)),
            pltpu.SemaphoreType.DMA((6,)),
            pltpu.SemaphoreType.DMA((16,)),
            pltpu.SemaphoreType.DMA((16,)),
        ],
        compiler_params=pltpu.CompilerParams(
            collective_id=0, has_side_effects=True, vmem_limit_bytes=VMEM_BYTES
        ),
        name="layer",
    )(
        lengths,
        cache,
        w_value,
        queries,
        sums,
        stats,
        w_out,
        residual,
        gain,
        w_gate,
        w_up,
        w_down,
    )


def solution(mesh):
    groups = mesh.shape["dp"]

    def on_device(
        query,
        latent_cache,
        lengths,
        w_uk,
        value_up_weight,
        w_out,
        residual,
        mlp_norm_scale,
        w_gate,
        w_up,
        w_down,
    ):
        cache = jnp.swapaxes(latent_cache, 1, 2)
        queries, sums, stats = attend_later(query, cache, lengths, w_uk)
        return layer(
            lengths,
            cache,
            value_up_weight,
            queries,
            sums,
            stats,
            w_out.T,
            residual.T,
            mlp_norm_scale,
            w_gate,
            w_up,
            w_down.T,
            groups,
            groups * mlp_norm_scale.shape[0],
        )

    return jax.shard_map(
        on_device,
        mesh=mesh,
        in_specs=(
            P("dp", "tp"),
            P("dp", None, None),
            P("dp"),
            P("tp", None, None),
            P("tp", None, None),
            P("tp", "dp"),
            P(None, "dp"),
            P("dp"),
            P("dp", "tp"),
            P("dp", "tp"),
            P("tp", "dp"),
        ),
        out_specs=P("tp", "dp"),
        check_vma=False,
    )
```
